256 devices in a mesh: space: 16 (over x, z_hi), mode: 16 (over y, z_lo, core).
Axes of the slice: x: 4, y: 4, z: 8 (z_hi: 4, z_lo: 2; z = z_hi * 2 + z_lo), core: 2. Of those that a mesh axis runs over, the one named last changes fastest.
Arguments:
- dist: bfloat16 [256, 2, 256, 576], P('mode', None, 'space')
- relax: float32 [2, 256], P(None, 'space'), may hold values from 0.1 to 0.9
- flags: int32 [2, 256], P(None, 'space'), may hold values from 0 to 2
- solid: int32 [2, 256], replicated, may hold values from 0 to 1, as said below
- inflow: bfloat16 [256, 576], P('mode'), may hold values from -2 to 2
- basis: bfloat16 [256, 256], replicated, as said below
- projection: bfloat16 [256, 256], replicated, may hold values from -0.375 to 0.375
Outputs:
- advanced: bfloat16 [256, 2, 256, 576], P('mode', None, 'space')
The draws below stay inside these ranges and needn't reach their ends.
Inputs may be any that keep to these rules, and one draw needn't show every extreme that they name: `solid`: 1 marks the cells of a disc whose centre lies in the band. `basis`: column 0 is all ones.
All inputs are finite; a program needn't handle non-finite values.
Results may differ from the reference program's by a relative error of at most 0.006.
The reference program's roundings to bfloat16 on the way count: a program that leaves them out, or rounds other values in their place, can miss the bound.
Values may be sent and summed in bfloat16 or wider, within the bound.
No kernel may reach another device: no remote copies, remote signals or barrier semaphores. Data moves between devices by JAX's collectives and lax.ppermute only.
A program may use at most 64 MiB of HBM per device.

```python
import math
import jax
import jax.numpy as jnp
from jax import lax

K = 256
Q = 256
VX = 24
V = 576
ROWS = 2
COLS_DEV = 16
COLS = 256


def draw_dist(key, part):
    key = jax.random.fold_in(key, 11)
    key_amp, key_noise, key_rough = jax.random.split(key, 3)
    index = jnp.arange(VX * VX)
    step = 9.2 / (VX - 1)
    velocity_horizontal = -4.6 + step * (index // VX).astype(jnp.float32)
    velocity_vertical = -4.6 + step * (index % VX).astype(jnp.float32)
    base = jnp.exp(-((velocity_horizontal - 0.5) ** 2 + velocity_vertical ** 2) / 2.0) / (2.0 * math.pi)
    shape = (K, ROWS, COLS, VX * VX)
    amp = jax.random.uniform(key_amp, (1, ROWS, COLS, 1), jnp.float32, 0.5, 1.5)
    noise = jax.random.normal(key_noise, shape, jnp.float32)
    rough = jax.random.uniform(key_rough, shape, jnp.float32, 0.7, 1.3)
    modes = jnp.arange(K)[:, None, None, None]
    density_field = jnp.where(modes == 0, amp * base * rough, 0.17 * base * noise)
    return density_field.astype(jnp.bfloat16)


def draw_basis(key, part):
    key = jax.random.fold_in(key, 23)
    values = jax.random.normal(key, (Q, K), jnp.float32)
    column = jnp.arange(K)[None, :]
    return jnp.where(column == 0, 1.0, values).astype(jnp.bfloat16)


def draw_solid(key, part):
    key = jax.random.fold_in(key, 37)
    key_x, key_y, key_r = jax.random.split(key, 3)
    centre_x = jax.random.randint(key_x, (), 0, COLS)
    centre_y = jax.random.randint(key_y, (), 0, ROWS)
    radius = jax.random.randint(key_r, (), 2, 2 * ROWS + 2)
    row_index = jnp.arange(ROWS)[:, None]
    col_index = jnp.arange(COLS)[None, :]
    inside = (col_index - centre_x) ** 2 + (row_index - centre_y) ** 2 <= radius * radius
    return inside.astype(jnp.int32)


def with_ends(array, rng, least, top_value):
    extent = array.shape
    place = [jax.random.randint(jax.random.fold_in(rng, axis), (), 0, extent[axis]) for axis in range(len(extent))]
    array = array.at[tuple(place)].set(least)
    longest = extent.index(max(extent))
    place[longest] = (place[longest] + 1) % extent[longest]
    return array.at[tuple(place)].set(top_value)


def levels(rng, shape, shards, smallest, top_value):
    factor_of, own = 1.0, jax.random.fold_in(rng, 6)
    for dim, shards_of in shards:
        steps = jnp.exp(jax.random.uniform(jax.random.fold_in(own, dim), (shards_of,), jnp.float32, smallest / len(shards), top_value / len(shards)))
        factor_of = factor_of * jnp.repeat(steps, shape[dim] // shards_of).reshape([-1 if axis == dim else 1 for axis in range(len(shape))])
    return factor_of


def scatter_about(stream_key, extent, spread, most, shards=(), held_as=jnp.bfloat16):
    values = jax.random.normal(stream_key, extent, jnp.float32) * spread
    if len(shards) > 0:
        values = levels(stream_key, extent, shards, -0.22, 0.18) * values
    return jnp.clip(values, min=-most, max=most).astype(held_as)


def setup_inputs(seed: int = 0) -> dict:
    keys = jax.random.split(jax.random.key(seed), 8)
    return {
        "dist": draw_dist(jax.random.fold_in(keys[7], 71), 0),
        "relax": jnp.clip(jnp.exp(math.log(0.9) - 2.1972245 * jax.random.uniform(keys[1], (ROWS, COLS), jnp.float32) ** levels(keys[1], (ROWS, COLS), ((1, 16),), -0.2, 0.2)), 0.1, 0.9),
        "flags": with_ends(jax.random.randint(keys[2], (ROWS, COLS), 0, 3), jax.random.fold_in(keys[2], 1), 0, 2).astype(jnp.int32),
        "solid": draw_solid(jax.random.fold_in(keys[7], 71), 0),
        "inflow": scatter_about(keys[4], (K, V), 0.15, 2.0, ((0, 16),)),
        "basis": draw_basis(jax.random.fold_in(keys[7], 71), 0),
        "projection": scatter_about(keys[6], (K, Q), Q ** -0.5, 0.375),
    }


VMAX = 4.6
DT_DX = 0.09
RHO_FLOOR = 0.3
TEMP_FLOOR = 0.2

def velocities(count):
    index = jnp.arange(count * count)
    step = 2.0 * VMAX / (count - 1)
    velocity_horizontal = -VMAX + step * (index // count).astype(jnp.float32)
    velocity_vertical = -VMAX + step * (index % count).astype(jnp.float32)
    return (velocity_horizontal, velocity_vertical, step * step)

def flip_axes(density_field, axes):
    shape = density_field.shape
    count = int(math.isqrt(shape[-1]))
    grid = density_field.reshape(shape[:-1] + (count, count))
    return jnp.flip(grid, axes).reshape(shape)

def maxwell(rho, mx, my, en, velocity_horizontal, velocity_vertical):
    safe = jnp.maximum(rho, RHO_FLOOR)
    ux = mx / safe
    uy = my / safe
    temp = jnp.maximum(en / safe - 0.5 * (ux * ux + uy * uy), TEMP_FLOOR)
    arg = ((velocity_horizontal - ux[..., None]) ** 2 + (velocity_vertical - uy[..., None]) ** 2) / (2.0 * temp[..., None])
    return (safe / (2.0 * math.pi * temp))[..., None] * jnp.exp(-arg)

def node_moments(node, velocity_horizontal, velocity_vertical, quadrature_weight):
    rho = quadrature_weight * lax.optimization_barrier(jnp.sum(node, -1))
    mx = quadrature_weight * lax.optimization_barrier(jnp.sum(node * velocity_horizontal, -1))
    my = quadrature_weight * lax.optimization_barrier(jnp.sum(node * velocity_vertical, -1))
    en = quadrature_weight * lax.optimization_barrier(jnp.sum(node * (0.5 * (velocity_horizontal * velocity_horizontal + velocity_vertical * velocity_vertical)), -1))
    return (rho, mx, my, en)

def collision_block(density_field, basis, projection, velocity_horizontal, velocity_vertical, quadrature_weight):
    node = jnp.einsum('qk,krcv->qrcv', basis.astype(jnp.float32), density_field.astype(jnp.float32), precision=lax.Precision.HIGHEST)
    rho, mx, my, en = node_moments(node, velocity_horizontal, velocity_vertical, quadrature_weight)
    equil = maxwell(rho, mx, my, en, velocity_horizontal, velocity_vertical).astype(jnp.bfloat16)
    out = jnp.einsum('kq,qrcv->krcv', projection.astype(jnp.float32), equil.astype(jnp.float32), precision=lax.Precision.HIGHEST)
    return out.astype(jnp.bfloat16)

def heun_update(padded_state, collision_term, relax, flags, padded_solid, inflow, first_column, column_total, velocity_horizontal, velocity_vertical):
    local_rows = padded_state[:, :, 1:-1].astype(jnp.float32)
    left = padded_state[:, :, :-2].astype(jnp.float32)
    right = padded_state[:, :, 2:].astype(jnp.float32)
    rows = local_rows.shape[1]
    cols = local_rows.shape[2]
    bounce = flip_axes(local_rows, (-2, -1))
    flag4 = flags[None, :, :, None]
    inflow4 = inflow.astype(jnp.float32)[:, None, None, :]
    edge_x = jnp.where(flag4 == 0, local_rows, jnp.where(flag4 == 1, inflow4, flip_axes(local_rows, (-2,))))
    edge_y = jnp.where(flag4 == 0, local_rows, jnp.where(flag4 == 1, inflow4, flip_axes(local_rows, (-1,))))
    column = first_column + jnp.arange(cols)
    out_left = (column == 0)[None, None, :, None]
    out_right = (column == column_total - 1)[None, None, :, None]
    solid_left = (padded_solid[:, :-2] == 1)[None, :, :, None]
    solid_right = (padded_solid[:, 2:] == 1)[None, :, :, None]
    left_val = jnp.where(out_left, edge_x, jnp.where(solid_left, bounce, left))
    right_val = jnp.where(out_right, edge_x, jnp.where(solid_right, bounce, right))
    up_x = jnp.where(velocity_horizontal > 0, left_val, right_val)
    zero_row = jnp.zeros_like(local_rows[:, :1])
    below = jnp.concatenate([zero_row, local_rows[:, :-1]], 1)
    above = jnp.concatenate([local_rows[:, 1:], zero_row], 1)
    solid_own = padded_solid[:, 1:-1]
    zero_mask = jnp.zeros((1, cols), solid_own.dtype)
    solid_below = (jnp.concatenate([zero_mask, solid_own[:-1]], 0) == 1)[None, :, :, None]
    solid_above = (jnp.concatenate([solid_own[1:], zero_mask], 0) == 1)[None, :, :, None]
    row_index = jnp.arange(rows)
    out_below = (row_index == 0)[None, :, None, None]
    out_above = (row_index == rows - 1)[None, :, None, None]
    below_val = jnp.where(out_below, edge_y, jnp.where(solid_below, bounce, below))
    above_val = jnp.where(out_above, edge_y, jnp.where(solid_above, bounce, above))
    up_y = jnp.where(velocity_vertical > 0, below_val, above_val)
    advect_upwind = -DT_DX * (jnp.abs(velocity_horizontal) * (local_rows - up_x) + jnp.abs(velocity_vertical) * (local_rows - up_y))
    state_delta = advect_upwind + relax[None, :, :, None] * (collision_term.astype(jnp.float32) - local_rows)
    retain_mask = (solid_own == 0)[None, :, :, None]
    return (local_rows + state_delta, retain_mask)

def reference(dist, relax, flags, solid, inflow, basis, projection):
    velocity_horizontal, velocity_vertical, quadrature_weight = velocities(VX)
    column_total = dist.shape[2]
    blocks = column_total // COLS_DEV
    padded_solid = jnp.pad(solid, ((0, 0), (1, 1)))

    def run_section(density_field, first):
        padded_all = jnp.pad(density_field, ((0, 0), (0, 0), (1, 1), (0, 0)))

        def one_block(block):
            begin_offset = (block * COLS_DEV).astype(jnp.int32)
            padded_state = lax.dynamic_slice_in_dim(padded_all, begin_offset, COLS_DEV + 2, 2)
            collision_term = collision_block(padded_state[:, :, 1:-1], basis, projection, velocity_horizontal, velocity_vertical, quadrature_weight)
            block_relaxation = lax.dynamic_slice_in_dim(relax, begin_offset, COLS_DEV, 1)
            block_flags = lax.dynamic_slice_in_dim(flags, begin_offset, COLS_DEV, 1)
            block_solid = lax.dynamic_slice_in_dim(padded_solid, begin_offset, COLS_DEV + 2, 1)
            after_step, retain_mask = heun_update(padded_state, collision_term, block_relaxation, block_flags, block_solid, inflow, begin_offset, column_total, velocity_horizontal, velocity_vertical)
            if first:
                result = after_step
            else:
                orig = lax.dynamic_slice_in_dim(dist, begin_offset, COLS_DEV, 2).astype(jnp.float32)
                result = 0.5 * orig + 0.5 * after_step
            return jnp.where(retain_mask, result, 0.0).astype(jnp.bfloat16)
        pieces = lax.map(one_block, jnp.arange(blocks, dtype=jnp.int32))
        pieces = jnp.moveaxis(pieces, 0, 2)
        return pieces.reshape(density_field.shape)
    section = run_section(dist, True)
    return run_section(section, False)
```

```python
import math

import numpy as np
import jax
import jax.numpy as jnp
from jax import lax
from jax.experimental import pallas as pl
from jax.experimental.pallas import tpu as pltpu
from jax.sharding import PartitionSpec as P

VX = 24
V = 576
ROWS = 2
COLS = 16
OWN = 32
MODES = 16
K = 256
VMAX = 4.6
DT_DX = 0.09
RHO_FLOOR = 0.3
TEMP_FLOOR = 0.2
STEP = 2.0 * VMAX / (VX - 1)
WEIGHT = STEP * STEP
HALF = 0.5 * STEP
LOG2E = math.log2(math.e)

HALO = 32
FAR = 36
BOUNCE = 40
MIRROR = 76
EDGE = 112
INFLOW = 116
SLOTS = 117

F32 = jnp.float32
BF16 = jnp.bfloat16
NT = (((1,), (1,)), ((), ()))
CHUNKS = tuple((128 * j, min(128, V - 128 * j)) for j in range(5))
LIMIT = 56 * 1024 * 1024


def tables():
    index = np.arange(V)
    a, b = index // VX, index % VX
    odd_a, odd_b = 2 * a - (VX - 1), 2 * b - (VX - 1)
    tri = (odd_a * odd_a - 1) // 8 + (odd_b * odd_b - 1) // 8
    weights = np.stack([np.ones(V), odd_a, odd_b, tri], 1)
    weights = np.repeat(weights, 32, axis=1)
    mirror = (a * VX + (VX - 1 - b))[:, None] == index[None, :]
    bounce = (V - 1 - index)[:, None] == index[None, :]
    rows = np.zeros((8, V), np.float32)
    rows[0] = DT_DX * np.abs(-VMAX + STEP * a)
    rows[1] = DT_DX * np.abs(-VMAX + STEP * b)
    rows[2] = (a >= VX // 2).astype(np.float32)
    rows[3] = (b >= VX // 2).astype(np.float32)
    return (
        jnp.asarray(weights.astype(np.float32), BF16),
        jnp.asarray(mirror.astype(np.float32), BF16),
        jnp.asarray(bounce.astype(np.float32), BF16),
        jnp.asarray(rows),
    )


def lanes(shape):
    return lax.broadcasted_iota(jnp.int32, shape, len(shape) - 1)


def pieces(value):
    hi = value.astype(BF16)
    rest = value - hi.astype(F32)
    mid = rest.astype(BF16)
    low = (rest - mid.astype(F32)).astype(BF16)
    return hi, mid, low


def edges_kernel(dist, relax, flags, cells, to_left, to_right, wide):
    for j, (at, n) in enumerate(CHUNKS):
        wide[j, :, :n] = dist[:, :, :, at : at + n].reshape(ROWS * COLS * MODES, n).astype(F32)

    def cell_chunk(cell, j):
        return wide[j, pl.ds(cell, MODES, stride=OWN), :]

    for cell in range(OWN):
        for j, (at, n) in enumerate(CHUNKS):
            cells[cell, :, at : at + n] = cell_chunk(cell, j)[:, :n].astype(BF16)
    lane = lanes((MODES, 128))
    for out, near, far, first in ((to_left, 0, 1, 0), (to_right, COLS - 1, COLS - 2, 2)):
        for r in range(ROWS):
            hi, mid, low = pieces(jnp.full((MODES, 128), relax[r, near], F32))
            flag = jnp.full((MODES, 128), flags[r, near], jnp.int32).astype(F32)
            extra = jnp.where(
                lane == 64,
                hi.astype(F32),
                jnp.where(
                    lane == 65,
                    mid.astype(F32),
                    jnp.where(lane == 66, low.astype(F32), jnp.where(lane == 67, flag, 0.0)),
                ),
            )
            for j in range(5):
                value = cell_chunk(r * COLS + near, j)
                if j == 4:
                    value = jnp.where(lane < 64, value, extra)
                out[r * 8 + j] = value.astype(BF16)
            for j in range(3):
                value = cell_chunk(r * COLS + far, first + j)
                if first + j == 4:
                    value = jnp.where(lane < 64, value, 0.0)
                out[r * 8 + 5 + j] = value.astype(BF16)


def mirrored(slots, held, cells, mirror, bounce):
    rows = cells * MODES
    turned = jnp.dot(held[:rows, :], mirror[...], preferred_element_type=F32)
    slots[MIRROR : MIRROR + cells] = turned.reshape(cells, MODES, V)
    for e, cell in enumerate((0, COLS - 1, COLS, 2 * COLS - 1)):
        held[rows + e * MODES : rows + (e + 1) * MODES, :] = turned[
            cell * MODES : (cell + 1) * MODES
        ].astype(BF16)
    back = jnp.dot(held[: rows + 64, :], bounce[...], preferred_element_type=F32)
    slots[BOUNCE : BOUNCE + cells] = back[:rows].reshape(cells, MODES, V)
    slots[EDGE : EDGE + 4] = back[rows:].reshape(4, MODES, V)


def advection(slots, rows, h, left, right, below, above):
    up_x = jnp.where(rows[2:3, :] > 0.5, left, right)
    up_y = jnp.where(rows[3:4, :] > 0.5, below, above)
    return rows[0:1, :] * (up_x - h) + rows[1:2, :] * (up_y - h)


def sources(r, c, column, flags, solid):
    own = r * COLS + c
    flag = flags[r, c]
    bounced = BOUNCE + own
    last = COLS * 16 - 1
    left = jnp.where(c == 0, HALO + r * 2, own - 1)
    right = jnp.where(c == COLS - 1, HALO + r * 2 + 1, own + 1)
    solid_left = solid[r, jnp.maximum(column - 1, 0)] == 1
    solid_right = solid[r, jnp.minimum(column + 1, last)] == 1

    def edge(turned):
        return jnp.where(flag == 0, own, jnp.where(flag == 1, INFLOW, turned))

    left = jnp.where(column == 0, edge(EDGE + r * 2), jnp.where(solid_left, bounced, left))
    right = jnp.where(
        column == last, edge(EDGE + r * 2 + 1), jnp.where(solid_right, bounced, right)
    )
    outside = edge(MIRROR + own)
    other = (1 - r) * COLS + c
    inside = jnp.where(solid[1 - r, column] == 1, bounced, other)
    below, above = (outside, inside) if r == 0 else (inside, outside)
    return left, right, below, above


def explicit_kernel(
    cells, from_left, from_right, inflow, relax, flags, solid, weights, mirror, bounce, rows,
    pay, base, slots, held, high, low,
):
    first = lax.axis_index("space") * COLS
    own = cells[...]
    slots[:OWN] = own.astype(F32)
    held[: OWN * MODES, :] = own.reshape(OWN * MODES, V)
    slots[INFLOW] = inflow[...].astype(F32)
    for side, ref, start in ((0, from_left, 2), (1, from_right, 0)):
        for r in range(ROWS):
            at_halo = HALO + r * 2 + side
            for j, (at, n) in enumerate(CHUNKS):
                value = ref[r * 8 + j][:, :n]
                slots[at_halo, :, at : at + n] = value.astype(F32)
                held[at_halo * MODES : (at_halo + 1) * MODES, at : at + n] = value
            for j in range(3):
                at, n = CHUNKS[start + j]
                slots[FAR + r * 2 + side, :, at : at + n] = ref[r * 8 + 5 + j][:, :n].astype(F32)
    mirrored(slots, held, 36, mirror, bounce)

    def own_cell(c, carry):
        for r in range(ROWS):
            cell = r * COLS + c
            column = first + c
            left, right, below, above = sources(r, c, column, flags, solid)
            h = slots[cell]
            moved = advection(
                slots, rows, h, slots[left], slots[right], slots[below], slots[above]
            )
            value = h - relax[r, c] * h + moved
            value = jnp.where(solid[r, column] == 0, value, 0.0)
            base[cell] = value
            hi = value.astype(BF16)
            at = pl.multiple_of(cell * MODES, MODES)
            high[pl.ds(at, MODES), :] = hi
            low[pl.ds(at, MODES), :] = (value - hi.astype(F32)).astype(BF16)
        return carry

    lax.fori_loop(0, COLS, own_cell, 0)
    for side, ref in ((0, from_left), (1, from_right)):
        for r in range(ROWS):
            cell = HALO + r * 2 + side
            column = jnp.clip(first - 1 if side == 0 else first + COLS, 1, COLS * 16 - 2)
            extra = ref[r * 8 + 4].astype(F32)
            rate = extra[:, 64:65] + extra[:, 65:66] + extra[:, 66:67]
            flag = extra[:, 67:68]
            h = slots[cell]
            edge = r * COLS + (0 if side == 0 else COLS - 1)
            far = FAR + r * 2 + side
            near_left, near_right = (far, edge) if side == 0 else (edge, far)
            bounced = BOUNCE + cell
            left = slots[jnp.where(solid[r, column - 1] == 1, bounced, near_left)]
            right = slots[jnp.where(solid[r, column + 1] == 1, bounced, near_right)]
            outside = jnp.where(
                flag < 0.5, h, jnp.where(flag < 1.5, slots[INFLOW], slots[MIRROR + cell])
            )
            inside = slots[
                jnp.where(solid[1 - r, column] == 1, bounced, HALO + (1 - r) * 2 + side)
            ]
            below, above = (outside, inside) if r == 0 else (inside, outside)
            value = h - rate * h + advection(slots, rows, h, left, right, below, above)
            base[cell] = jnp.where(solid[r, column] == 0, value, 0.0)

    place = lanes((MODES, 128)) % 32

    def fold(sums, cell_list):
        total = jnp.zeros((MODES, 128), F32)
        for i, cell in enumerate(cell_list):
            total += jnp.where(place == i, sums[cell * MODES : (cell + 1) * MODES], 0.0)
        return total

    sums = jnp.dot(held[: 36 * MODES, :], weights[...], preferred_element_type=F32)
    next_sums = jnp.dot(high[...], weights[...], preferred_element_type=F32) + jnp.dot(
        low[...], weights[...], preferred_element_type=F32
    )
    out = (
        fold(sums, range(OWN)),
        fold(next_sums, range(OWN)),
        fold(sums, range(HALO, HALO + 4)),
    )
    for d in range(16):
        for i in range(3):
            pay[d, :, 128 * i : 128 * (i + 1)] = out[i]


def exact_nt(value, table):
    total = None
    for piece in pieces(value):
        part = lax.dot_general(piece, table, NT, preferred_element_type=F32)
        total = part if total is None else total + part
    return total


def set_parameters(par, at, sums):
    s0, s1, s2, s3 = sums
    n = s0.shape[0]
    rho = WEIGHT * s0
    mx = (WEIGHT * HALF) * s1
    my = (WEIGHT * HALF) * s2
    en = (WEIGHT * HALF * HALF) * (4.0 * s3 + s0)
    safe = jnp.maximum(rho, RHO_FLOOR)
    ux = mx / safe
    uy = my / safe
    temp = jnp.maximum(en / safe - 0.5 * (ux * ux + uy * uy), TEMP_FLOOR)
    par[0, at : at + n] = ux
    par[1, at : at + n] = uy
    par[2, at : at + n] = (-0.5 * LOG2E) / temp
    par[3, at : at + n] = safe / (2.0 * math.pi * temp)


def factors(par, cell):
    ux = par[0, pl.ds(cell, 1), :]
    uy = par[1, pl.ds(cell, 1), :]
    rate = par[2, pl.ds(cell, 1), :]
    scale = par[3, pl.ds(cell, 1), :]
    speed = lax.broadcasted_iota(jnp.int32, (VX, K), 0).astype(F32) * STEP - VMAX
    dx = speed - ux
    dy = speed - uy
    return scale * jnp.exp2(dx * dx * rate), jnp.exp2(dy * dy * rate)


def project(along_x, along_y, equil, projection):
    for i in range(VX // 2):
        pair = jnp.concatenate(
            [along_x[2 * i : 2 * i + 1] * along_y, along_x[2 * i + 1 : 2 * i + 2] * along_y], 0
        )
        equil[48 * i : 48 * (i + 1), :] = pair.astype(BF16)
    out = lax.dot_general(projection, equil[...], NT, preferred_element_type=F32)
    return out.astype(BF16).astype(F32)


def collide_kernel(
    gathered, basis, projection, base, cells, from_left, from_right, inflow, relax, flags, solid,
    mirror, bounce, rows,
    out, slots, held, par, sums1, equil, wide,
):
    first = lax.axis_index("space") * COLS
    mode = lax.axis_index("mode") * MODES
    mine = projection[pl.ds(pl.multiple_of(mode, MODES), MODES), :]
    turned = gathered[...].T
    node = exact_nt(turned[:128], basis[...])
    halo_node = exact_nt(turned[256:384], basis[...])
    set_parameters(par, 0, [node[32 * i : 32 * i + 32] for i in range(4)])
    set_parameters(par, 32, [halo_node[32 * i : 32 * i + 8] for i in range(4)])
    slots[INFLOW] = inflow[...].astype(F32)

    odd = (2 * lax.broadcasted_iota(jnp.int32, (VX, K), 0) - (VX - 1)).astype(F32)
    tri = (odd * odd - 1.0) * 0.125

    def sums_of(value):
        return (
            jnp.sum(value, 0, keepdims=True),
            jnp.sum(value * odd, 0, keepdims=True),
            jnp.sum(value * tri, 0, keepdims=True),
        )

    def first_stage(c, carry):
        for r in range(ROWS):
            cell = r * COLS + c
            along_x, along_y = factors(par, cell)
            coll = project(along_x, along_y, equil.at[r], mine)
            fluid = solid[r, first + c] == 0
            rate = jnp.where(fluid, relax[r, c], 0.0)
            section = (base[cell] + rate * coll).astype(BF16)
            slots[cell] = section.astype(F32)
            held[pl.ds(pl.multiple_of(cell * MODES, MODES), MODES), :] = section
            x0, x1, x2 = sums_of(along_x)
            y0, y1, y2 = sums_of(along_y)
            y0, y1, y2 = rate * y0, rate * y1, rate * y2
            sums1[pl.ds(cell, 1), :] = x0 * y0
            sums1[pl.ds(32 + cell, 1), :] = x1 * y0
            sums1[pl.ds(64 + cell, 1), :] = x0 * y1
            sums1[pl.ds(96 + cell, 1), :] = x2 * y0 + x0 * y2
        return carry

    lax.fori_loop(0, COLS, first_stage, 0)
    for side, ref in ((0, from_left), (1, from_right)):
        for r in range(ROWS):
            cell = HALO + r * 2 + side
            column = jnp.clip(first - 1 if side == 0 else first + COLS, 0, COLS * 16 - 1)
            extra = ref[r * 8 + 4].astype(F32)
            rate = extra[:, 64:65] + extra[:, 65:66] + extra[:, 66:67]
            rate = jnp.where(solid[r, column] == 0, rate, 0.0)
            along_x, along_y = factors(par, cell)
            coll = project(along_x, along_y, equil.at[r], mine)
            slots[cell] = (base[cell] + rate * coll).astype(BF16).astype(F32)

    mirrored(slots, held, 32, mirror, bounce)
    mixed = turned[128:256] + exact_nt(sums1[...], projection[...])
    node = exact_nt(mixed, basis[...])
    set_parameters(par, 0, [node[32 * i : 32 * i + 32] for i in range(4)])

    def second_stage(c, carry):
        for r in range(ROWS):
            cell = r * COLS + c
            column = first + c
            along_x, along_y = factors(par, cell)
            coll = project(along_x, along_y, equil.at[r], mine)
            left, right, below, above = sources(r, c, column, flags, solid)
            h = slots[cell]
            moved = advection(
                slots, rows, h, slots[left], slots[right], slots[below], slots[above]
            )
            value = h + moved + relax[r, c] * (coll - h)
            value = 0.5 * cells[cell].astype(F32) + 0.5 * value
            value = jnp.where(solid[r, column] == 0, value, 0.0)
            for j, (at, n) in enumerate(CHUNKS):
                wide[j, pl.ds(cell, MODES, stride=OWN), :n] = value[:, at : at + n]
        return carry

    lax.fori_loop(0, COLS, second_stage, 0)
    for j, (at, n) in enumerate(CHUNKS):
        out[:, :, :, at : at + n] = (
            wide[j, :, :n].astype(BF16).reshape(MODES, ROWS, COLS, n)
        )


def on_device(dist, relax, flags, solid, inflow, basis, projection):
    weights, mirror, bounce, rows = tables()
    vmem = pl.BlockSpec(memory_space=pltpu.VMEM)
    smem = pl.BlockSpec(memory_space=pltpu.SMEM)
    params = pltpu.CompilerParams(vmem_limit_bytes=LIMIT)

    cells, to_left, to_right = pl.pallas_call(
        edges_kernel,
        out_shape=(
            jax.ShapeDtypeStruct((OWN, MODES, V), BF16),
            jax.ShapeDtypeStruct((16, MODES, 128), BF16),
            jax.ShapeDtypeStruct((16, MODES, 128), BF16),
        ),
        in_specs=[vmem, smem, smem],
        out_specs=(vmem, vmem, vmem),
        scratch_shapes=[pltpu.VMEM((5, OWN * MODES, 128), F32)],
        compiler_params=params,
    )(dist, relax, flags)
    count = lax.axis_size("space")
    from_left = lax.ppermute(to_right, "space", [(i, (i + 1) % count) for i in range(count)])
    from_right = lax.ppermute(to_left, "space", [((i + 1) % count, i) for i in range(count)])

    pay, base = pl.pallas_call(
        explicit_kernel,
        out_shape=(
            jax.ShapeDtypeStruct((16, MODES, 384), F32),
            jax.ShapeDtypeStruct((36, MODES, V), F32),
        ),
        in_specs=[vmem] * 4 + [smem] * 3 + [vmem] * 4,
        out_specs=(vmem, vmem),
        scratch_shapes=[
            pltpu.VMEM((SLOTS, MODES, V), F32),
            pltpu.VMEM((640, V), BF16),
            pltpu.VMEM((OWN * MODES, V), BF16),
            pltpu.VMEM((OWN * MODES, V), BF16),
        ],
        compiler_params=params,
    )(cells, from_left, from_right, inflow, relax, flags, solid, weights, mirror, bounce, rows)
    gathered = lax.all_to_all(pay, "mode", split_axis=0, concat_axis=0, tiled=True)
    gathered = gathered.reshape(K, 384)

    return pl.pallas_call(
        collide_kernel,
        out_shape=jax.ShapeDtypeStruct((MODES, ROWS, COLS, V), BF16),
        in_specs=[vmem] * 8 + [smem] * 3 + [vmem] * 3,
        out_specs=vmem,
        scratch_shapes=[
            pltpu.VMEM((SLOTS, MODES, V), F32),
            pltpu.VMEM((576, V), BF16),
            pltpu.VMEM((4, 40, K), F32),
            pltpu.VMEM((128, K), F32),
            pltpu.VMEM((2, V, K), BF16),
            pltpu.VMEM((5, OWN * MODES, 128), F32),
        ],
        compiler_params=params,
    )(
        gathered, basis, projection, base, cells, from_left, from_right, inflow,
        relax, flags, solid, mirror, bounce, rows,
    )


def solution(mesh):
    placed = (
        P("mode", None, "space", None),
        P(None, "space"),
        P(None, "space"),
        P(),
        P("mode", None),
        P(),
        P(),
    )
    return jax.shard_map(
        on_device,
        mesh=mesh,
        in_specs=placed,
        out_specs=P("mode", None, "space", None),
        check_vma=False,
    )
```

```python
import math

import numpy as np
import jax
import jax.numpy as jnp
from jax import lax
from jax.experimental import pallas as pl
from jax.experimental.pallas import tpu as pltpu
from jax.sharding import PartitionSpec as P

VX = 24
V = 576
ROWS = 2
COLS = 16
OWN = 32
MODES = 16
K = 256
VMAX = 4.6
DT_DX = 0.09
RHO_FLOOR = 0.3
TEMP_FLOOR = 0.2
STEP = 2.0 * VMAX / (VX - 1)
WEIGHT = STEP * STEP
HALF = 0.5 * STEP
LOG2E = math.log2(math.e)

HALO = 32
FAR = 36
BOUNCE = 40
MIRROR = 76
EDGE = 112
INFLOW = 116
SLOTS = 117

F32 = jnp.float32
BF16 = jnp.bfloat16
NT = (((1,), (1,)), ((), ()))
CHUNKS = tuple((128 * j, min(128, V - 128 * j)) for j in range(5))
LIMIT = 56 * 1024 * 1024


def tables():
    index = np.arange(V)
    a, b = index // VX, index % VX
    odd_a, odd_b = 2 * a - (VX - 1), 2 * b - (VX - 1)
    tri = (odd_a * odd_a - 1) // 8 + (odd_b * odd_b - 1) // 8
    weights = np.stack([np.ones(V), odd_a, odd_b, tri], 1)
    weights = np.repeat(weights, 32, axis=1)
    turned = a * VX + (VX - 1 - b)
    swap = np.zeros((1152, 128), np.float32)
    lane = np.arange(128)
    swap[191 - lane, lane] = 1.0
    for at, left, out in ((256, 0, 0), (512, 0, 128), (896, 128, 256)):
        swap[at + turned[out + lane] - left, lane] = 1.0
    rows = np.zeros((8, V), np.float32)
    rows[0] = DT_DX * np.abs(-VMAX + STEP * a)
    rows[1] = DT_DX * np.abs(-VMAX + STEP * b)
    rows[2] = (a >= VX // 2).astype(np.float32)
    rows[3] = (b >= VX // 2).astype(np.float32)
    return (
        jnp.asarray(weights.astype(np.float32), BF16),
        jnp.asarray(swap, BF16),
        jnp.asarray(rows),
    )


def lanes(shape):
    return lax.broadcasted_iota(jnp.int32, shape, len(shape) - 1)


def pieces(value):
    hi = value.astype(BF16)
    rest = value - hi.astype(F32)
    mid = rest.astype(BF16)
    low = (rest - mid.astype(F32)).astype(BF16)
    return hi, mid, low


def cell_chunk(wide, cell, j):
    return wide[j, pl.ds(cell, MODES, stride=OWN), :]


def widen(dist, wide):
    for j, (at, n) in enumerate(CHUNKS):
        wide[j, :, :n] = dist[:, :, :, at : at + n].reshape(ROWS * COLS * MODES, n).astype(F32)


def edges_kernel(dist, relax, flags, to_left, to_right, wide):
    widen(dist, wide)
    lane = lanes((MODES, 128))
    for out, near, far, first in ((to_left, 0, 1, 0), (to_right, COLS - 1, COLS - 2, 2)):
        for r in range(ROWS):
            hi, mid, low = pieces(jnp.full((MODES, 128), relax[r, near], F32))
            flag = jnp.full((MODES, 128), flags[r, near], jnp.int32).astype(F32)
            extra = jnp.where(
                lane == 64,
                hi.astype(F32),
                jnp.where(
                    lane == 65,
                    mid.astype(F32),
                    jnp.where(lane == 66, low.astype(F32), jnp.where(lane == 67, flag, 0.0)),
                ),
            )
            for j in range(5):
                value = cell_chunk(wide, r * COLS + near, j)
                if j == 4:
                    value = jnp.where(lane < 64, value, extra)
                out[r * 8 + j] = value.astype(BF16)
            for j in range(3):
                value = cell_chunk(wide, r * COLS + far, first + j)
                if first + j == 4:
                    value = jnp.where(lane < 64, value, 0.0)
                out[r * 8 + 5 + j] = value.astype(BF16)


def turn(held, count, swap):
    parts = ((0, 256, 256, 128), (0, 384, 512, 128), (128, 256, 896, 128), (384, 192, 256, 128), (384, 192, 512, 64))
    return permuted(held, count, swap, parts)


def reverse(held, count, swap):
    parts = ((384, 192, 0, 128), (256, 256, 0, 128), (128, 256, 0, 128), (0, 256, 0, 128), (0, 128, 128, 64))
    return permuted(held, count, swap, parts)


def permuted(held, count, swap, parts):
    return [
        jnp.dot(held[:count, lane : lane + n], swap[at : at + n, :width], preferred_element_type=F32)
        for lane, n, at, width in parts
    ]


def mirrored(slots, held, cells, swap):
    rows = cells * MODES
    for (at, n), part in zip(CHUNKS, turn(held, rows, swap)):
        slots[MIRROR : MIRROR + cells, :, at : at + n] = part.reshape(cells, MODES, n)
        for e, cell in enumerate((0, COLS - 1, COLS, 2 * COLS - 1)):
            held[rows + e * MODES : rows + (e + 1) * MODES, at : at + n] = part[
                cell * MODES : (cell + 1) * MODES
            ].astype(BF16)
    for (at, n), part in zip(CHUNKS, reverse(held, rows + 64, swap)):
        slots[BOUNCE : BOUNCE + cells, :, at : at + n] = part[:rows].reshape(cells, MODES, n)
        slots[EDGE : EDGE + 4, :, at : at + n] = part[rows:].reshape(4, MODES, n)


def advection(slots, rows, h, left, right, below, above):
    up_x = jnp.where(rows[2:3, :] > 0.5, left, right)
    up_y = jnp.where(rows[3:4, :] > 0.5, below, above)
    return rows[0:1, :] * (up_x - h) + rows[1:2, :] * (up_y - h)


def sources(r, c, column, flags, solid):
    own = r * COLS + c
    flag = flags[r, c]
    bounced = BOUNCE + own
    last = COLS * 16 - 1
    left = jnp.where(c == 0, HALO + r * 2, own - 1)
    right = jnp.where(c == COLS - 1, HALO + r * 2 + 1, own + 1)
    solid_left = solid[r, jnp.maximum(column - 1, 0)] == 1
    solid_right = solid[r, jnp.minimum(column + 1, last)] == 1

    def edge(turned):
        return jnp.where(flag == 0, own, jnp.where(flag == 1, INFLOW, turned))

    left = jnp.where(column == 0, edge(EDGE + r * 2), jnp.where(solid_left, bounced, left))
    right = jnp.where(
        column == last, edge(EDGE + r * 2 + 1), jnp.where(solid_right, bounced, right)
    )
    outside = edge(MIRROR + own)
    other = (1 - r) * COLS + c
    inside = jnp.where(solid[1 - r, column] == 1, bounced, other)
    below, above = (outside, inside) if r == 0 else (inside, outside)
    return left, right, below, above


def fold(sums, count):
    place = lanes((MODES, 128)) % 32
    total = jnp.zeros((MODES, 128), F32)
    for i in range(count):
        total += jnp.where(place == i, sums[i * MODES : (i + 1) * MODES], 0.0)
    return total


def split(value, high, low, cell):
    hi = value.astype(BF16)
    at = pl.multiple_of(cell * MODES, MODES)
    high[pl.ds(at, MODES), :] = hi
    low[pl.ds(at, MODES), :] = (value - hi.astype(F32)).astype(BF16)


def explicit_kernel(
    dist, inflow, relax, flags, solid, weights, swap, rows,
    cells, ends, base, sums, wide, slots, held, high, low,
):
    first = lax.axis_index("space") * COLS
    widen(dist, wide)

    def gather(c, carry):
        for r in range(ROWS):
            cell = r * COLS + c
            at_held = pl.multiple_of(cell * MODES, MODES)
            for j, (at, n) in enumerate(CHUNKS):
                value = cell_chunk(wide, cell, j)[:, :n]
                slots[cell, :, at : at + n] = value
                held[pl.ds(at_held, MODES), at : at + n] = value.astype(BF16)
        return carry

    lax.fori_loop(0, COLS, gather, 0, unroll=2)
    cells[...] = held[: OWN * MODES, :].reshape(OWN, MODES, V)
    for e, cell in enumerate((0, COLS - 1, COLS, 2 * COLS - 1)):
        ends[e] = held[cell * MODES : (cell + 1) * MODES, :]
    slots[INFLOW] = inflow[...].astype(F32)
    slots[HALO : HALO + 4] = jnp.zeros((4, MODES, V), F32)
    mirrored(slots, held, OWN, swap)

    def own_cell(c, carry):
        for r in range(ROWS):
            cell = r * COLS + c
            column = first + c
            left, right, below, above = sources(r, c, column, flags, solid)
            h = slots[cell]
            moved = advection(
                slots, rows, h, slots[left], slots[right], slots[below], slots[above]
            )
            value = h - relax[r, c] * h + moved
            value = jnp.where(solid[r, column] == 0, value, 0.0)
            base[cell] = value
            split(value, high, low, cell)
        return carry

    lax.fori_loop(0, COLS, own_cell, 0, unroll=4)
    sums[0] = fold(
        jnp.dot(held[: OWN * MODES, :], weights[...], preferred_element_type=F32), OWN
    )
    sums[1] = fold(
        jnp.dot(high[...], weights[...], preferred_element_type=F32)
        + jnp.dot(low[...], weights[...], preferred_element_type=F32),
        OWN,
    )


def halo_kernel(
    ends, from_left, from_right, sums, inflow, solid, weights, swap, rows,
    pay, edge, near, far, turned, back, held,
):
    first = lax.axis_index("space") * COLS
    last = COLS * 16 - 1
    for side, ref, start in ((0, from_left, 2), (1, from_right, 0)):
        for r in range(ROWS):
            i = r * 2 + side
            for j, (at, n) in enumerate(CHUNKS):
                value = ref[r * 8 + j][:, :n]
                near[i, :, at : at + n] = value.astype(F32)
                held[i * MODES : (i + 1) * MODES, at : at + n] = value
            for j in range(3):
                at, n = CHUNKS[start + j]
                far[i, :, at : at + n] = ref[r * 8 + 5 + j][:, :n].astype(F32)
    for (at, n), part in zip(CHUNKS, turn(held, 64, swap)):
        turned[:, :, at : at + n] = part.reshape(4, MODES, n)
    for (at, n), part in zip(CHUNKS, reverse(held, 64, swap)):
        back[:, :, at : at + n] = part.reshape(4, MODES, n)
    source = inflow[...].astype(F32)
    for side, ref in ((0, from_left), (1, from_right)):
        for r in range(ROWS):
            i = r * 2 + side
            beyond = first - 1 if side == 0 else first + COLS
            column = jnp.clip(beyond, 1, last - 1)
            extra = ref[r * 8 + 4].astype(F32)
            rate = extra[:, 64:65] + extra[:, 65:66] + extra[:, 66:67]
            flag = extra[:, 67:68]
            h = near[i]
            own = ends[i].astype(F32)
            bounced = back[i]
            left, right = (far[i], own) if side == 0 else (own, far[i])
            left = jnp.where(solid[r, column - 1] == 1, bounced, left)
            right = jnp.where(solid[r, column + 1] == 1, bounced, right)
            outside = jnp.where(flag < 0.5, h, jnp.where(flag < 1.5, source, turned[i]))
            inside = jnp.where(solid[1 - r, column] == 1, bounced, near[(1 - r) * 2 + side])
            below, above = (outside, inside) if r == 0 else (inside, outside)
            value = h - rate * h + advection(None, rows, h, left, right, below, above)
            edge[4 + i] = jnp.where(solid[r, column] == 0, value, 0.0)

            inner = first if side == 0 else first + COLS - 1
            inside_band = (beyond >= 0) & (beyond <= last)
            used = inside_band & (solid[r, jnp.clip(beyond, 0, last)] == 0) & (solid[r, inner] == 0)
            taken = rows[2:3, :] > 0.5 if side == 0 else rows[2:3, :] < 0.5
            value = jnp.where(taken, rows[0:1, :] * h, 0.0)
            value = jnp.where(used, value, 0.0)
            edge[i] = value
            hi = value.astype(BF16)
            held[64 + i * MODES : 80 + i * MODES, :] = hi
            held[128 + i * MODES : 144 + i * MODES, :] = (value - hi.astype(F32)).astype(BF16)
    edge[8] = jnp.zeros((MODES, V), F32)
    folded = jnp.dot(held[...], weights[...], preferred_element_type=F32)
    place = lanes((MODES, 128)) % 32
    added = folded[64:128] + folded[128:]
    later = sums[1]
    for i in range(4):
        cell = (i // 2) * COLS + (0 if i % 2 == 0 else COLS - 1)
        later += jnp.where(place == cell, added[i * MODES : (i + 1) * MODES], 0.0)
    out = (sums[0], later, fold(folded, 4))
    for d in range(16):
        for i in range(3):
            pay[d, :, 128 * i : 128 * (i + 1)] = out[i]


def exact_nt(value, table):
    total = None
    for piece in pieces(value):
        part = lax.dot_general(piece, table, NT, preferred_element_type=F32)
        total = part if total is None else total + part
    return total


def set_parameters(par, at, sums):
    s0, s1, s2, s3 = sums
    n = s0.shape[0]
    rho = WEIGHT * s0
    mx = (WEIGHT * HALF) * s1
    my = (WEIGHT * HALF) * s2
    en = (WEIGHT * HALF * HALF) * (4.0 * s3 + s0)
    safe = jnp.maximum(rho, RHO_FLOOR)
    ux = mx / safe
    uy = my / safe
    temp = jnp.maximum(en / safe - 0.5 * (ux * ux + uy * uy), TEMP_FLOOR)
    par[0, at : at + n] = ux
    par[1, at : at + n] = uy
    par[2, at : at + n] = (-0.5 * LOG2E) / temp
    par[3, at : at + n] = safe / (2.0 * math.pi * temp)


def factors(par, cell):
    ux = par[0, pl.ds(cell, 1), :]
    uy = par[1, pl.ds(cell, 1), :]
    rate = par[2, pl.ds(cell, 1), :]
    scale = par[3, pl.ds(cell, 1), :]
    speed = lax.broadcasted_iota(jnp.int32, (VX, K), 0).astype(F32) * STEP - VMAX
    dx = speed - ux
    dy = speed - uy
    return scale * jnp.exp2(dx * dx * rate), jnp.exp2(dy * dy * rate)


def project(along_x, along_y, equil, projection):
    for i in range(VX // 2):
        pair = jnp.concatenate(
            [along_x[2 * i : 2 * i + 1] * along_y, along_x[2 * i + 1 : 2 * i + 2] * along_y], 0
        )
        equil[48 * i : 48 * (i + 1), :] = pair.astype(BF16)
    out = lax.dot_general(projection, equil[...], NT, preferred_element_type=F32)
    return out.astype(BF16).astype(F32)


def collide_kernel(
    gathered, basis, projection, base_far, edge_far, cells_far, from_left, from_right, inflow,
    relax, flags, solid, swap_far, rows,
    out, slots, held, par, sums1, equil, wide, base, edge, cells, swap, arrived,
):
    copies = [
        pltpu.make_async_copy(source, target, arrived.at[i])
        for i, (source, target) in enumerate(
            ((base_far, base), (edge_far, edge), (cells_far, cells), (swap_far, swap))
        )
    ]
    for copy in copies:
        copy.start()
    first = lax.axis_index("space") * COLS
    mode = lax.axis_index("mode") * MODES
    mine = projection[pl.ds(pl.multiple_of(mode, MODES), MODES), :]
    turned = gathered[...].T
    node = exact_nt(turned[:128], basis[...])
    halo_node = exact_nt(turned[256:384], basis[...])
    set_parameters(par, 0, [node[32 * i : 32 * i + 32] for i in range(4)])
    set_parameters(par, 32, [halo_node[32 * i : 32 * i + 8] for i in range(4)])
    slots[INFLOW] = inflow[...].astype(F32)

    odd = (2 * lax.broadcasted_iota(jnp.int32, (VX, K), 0) - (VX - 1)).astype(F32)
    tri = (odd * odd - 1.0) * 0.125

    def sums_of(value):
        return (
            jnp.sum(value, 0, keepdims=True),
            jnp.sum(value * odd, 0, keepdims=True),
            jnp.sum(value * tri, 0, keepdims=True),
        )

    def first_stage(c, carry):
        for r in range(ROWS):
            cell = r * COLS + c
            along_x, along_y = factors(par, cell)
            coll = project(along_x, along_y, equil.at[r], mine)
            fluid = solid[r, first + c] == 0
            rate = jnp.where(fluid, relax[r, c], 0.0)
            end = jnp.where(c == 0, r * 2, jnp.where(c == COLS - 1, r * 2 + 1, 8))
            section = (base[cell] + edge[end] + rate * coll).astype(BF16)
            slots[cell] = section.astype(F32)
            held[pl.ds(pl.multiple_of(cell * MODES, MODES), MODES), :] = section
            x0, x1, x2 = sums_of(along_x)
            y0, y1, y2 = sums_of(along_y)
            y0, y1, y2 = rate * y0, rate * y1, rate * y2
            sums1[pl.ds(cell, 1), :] = x0 * y0
            sums1[pl.ds(32 + cell, 1), :] = x1 * y0
            sums1[pl.ds(64 + cell, 1), :] = x0 * y1
            sums1[pl.ds(96 + cell, 1), :] = x2 * y0 + x0 * y2
        return carry

    for copy in copies:
        copy.wait()
    lax.fori_loop(0, COLS, first_stage, 0, unroll=4)
    for side, ref in ((0, from_left), (1, from_right)):
        for r in range(ROWS):
            cell = HALO + r * 2 + side
            column = jnp.clip(first - 1 if side == 0 else first + COLS, 0, COLS * 16 - 1)
            extra = ref[r * 8 + 4].astype(F32)
            rate = extra[:, 64:65] + extra[:, 65:66] + extra[:, 66:67]
            rate = jnp.where(solid[r, column] == 0, rate, 0.0)
            along_x, along_y = factors(par, cell)
            coll = project(along_x, along_y, equil.at[r], mine)
            slots[cell] = (edge[4 + r * 2 + side] + rate * coll).astype(BF16).astype(F32)

    mirrored(slots, held, OWN, swap)
    mixed = turned[128:256] + exact_nt(sums1[...], projection[...])
    node = exact_nt(mixed, basis[...])
    set_parameters(par, 0, [node[32 * i : 32 * i + 32] for i in range(4)])

    def second_stage(c, carry):
        for r in range(ROWS):
            cell = r * COLS + c
            column = first + c
            along_x, along_y = factors(par, cell)
            coll = project(along_x, along_y, equil.at[r], mine)
            left, right, below, above = sources(r, c, column, flags, solid)
            h = slots[cell]
            moved = advection(
                slots, rows, h, slots[left], slots[right], slots[below], slots[above]
            )
            value = h + moved + relax[r, c] * (coll - h)
            value = 0.5 * cells[cell].astype(F32) + 0.5 * value
            value = jnp.where(solid[r, column] == 0, value, 0.0)
            for j, (at, n) in enumerate(CHUNKS):
                wide[j, pl.ds(cell, MODES, stride=OWN), :n] = value[:, at : at + n]
        return carry

    lax.fori_loop(0, COLS, second_stage, 0, unroll=4)
    for j, (at, n) in enumerate(CHUNKS):
        out[:, :, :, at : at + n] = (
            wide[j, :, :n].astype(BF16).reshape(MODES, ROWS, COLS, n)
        )


def on_device(dist, relax, flags, solid, inflow, basis, projection):
    weights, swap, rows = tables()
    vmem = pl.BlockSpec(memory_space=pltpu.VMEM)
    smem = pl.BlockSpec(memory_space=pltpu.SMEM)
    far = pl.BlockSpec(memory_space=pl.ANY)
    params = pltpu.CompilerParams(vmem_limit_bytes=LIMIT)

    to_left, to_right = pl.pallas_call(
        edges_kernel,
        out_shape=(
            jax.ShapeDtypeStruct((16, MODES, 128), BF16),
            jax.ShapeDtypeStruct((16, MODES, 128), BF16),
        ),
        in_specs=[vmem, smem, smem],
        out_specs=(vmem, vmem),
        scratch_shapes=[pltpu.VMEM((5, OWN * MODES, 128), F32)],
        compiler_params=params,
    )(dist, relax, flags)
    count = lax.axis_size("space")
    from_left = lax.ppermute(to_right, "space", [(i, (i + 1) % count) for i in range(count)])
    from_right = lax.ppermute(to_left, "space", [((i + 1) % count, i) for i in range(count)])

    cells, ends, base, sums = pl.pallas_call(
        explicit_kernel,
        out_shape=(
            jax.ShapeDtypeStruct((OWN, MODES, V), BF16),
            jax.ShapeDtypeStruct((4, MODES, V), BF16),
            jax.ShapeDtypeStruct((OWN, MODES, V), F32),
            jax.ShapeDtypeStruct((2, MODES, 128), F32),
        ),
        in_specs=[vmem] * 2 + [smem] * 3 + [vmem] * 3,
        out_specs=(vmem, vmem, vmem, vmem),
        scratch_shapes=[
            pltpu.VMEM((5, OWN * MODES, 128), F32),
            pltpu.VMEM((SLOTS, MODES, V), F32),
            pltpu.VMEM((576, V), BF16),
            pltpu.VMEM((OWN * MODES, V), BF16),
            pltpu.VMEM((OWN * MODES, V), BF16),
        ],
        compiler_params=params,
        cost_estimate=pl.CostEstimate(
            flops=20_000_000_000, bytes_accessed=4_000_000, transcendentals=0
        ),
    )(dist, inflow, relax, flags, solid, weights, swap, rows)

    pay, edge = pl.pallas_call(
        halo_kernel,
        out_shape=(
            jax.ShapeDtypeStruct((16, MODES, 384), F32),
            jax.ShapeDtypeStruct((9, MODES, V), F32),
        ),
        in_specs=[vmem] * 5 + [smem] + [vmem] * 3,
        out_specs=(vmem, vmem),
        scratch_shapes=[pltpu.VMEM((4, MODES, V), F32)] * 4 + [pltpu.VMEM((192, V), BF16)],
        compiler_params=params,
    )(ends, from_left, from_right, sums, inflow, solid, weights, swap, rows)
    gathered = lax.all_to_all(pay, "mode", split_axis=0, concat_axis=0, tiled=True)
    gathered = gathered.reshape(K, 384)

    return pl.pallas_call(
        collide_kernel,
        out_shape=jax.ShapeDtypeStruct((MODES, ROWS, COLS, V), BF16),
        in_specs=[vmem] * 3 + [far] * 3 + [vmem] * 3 + [smem] * 3 + [far, vmem],
        out_specs=vmem,
        scratch_shapes=[
            pltpu.VMEM((SLOTS, MODES, V), F32),
            pltpu.VMEM((576, V), BF16),
            pltpu.VMEM((4, 40, K), F32),
            pltpu.VMEM((128, K), F32),
            pltpu.VMEM((2, V, K), BF16),
            pltpu.VMEM((5, OWN * MODES, 128), F32),
            pltpu.VMEM((OWN, MODES, V), F32),
            pltpu.VMEM((9, MODES, V), F32),
            pltpu.VMEM((OWN, MODES, V), BF16),
            pltpu.VMEM((1152, 128), BF16),
            pltpu.SemaphoreType.DMA((4,)),
        ],
        compiler_params=params,
    )(
        gathered, basis, projection, base, edge, cells, from_left, from_right, inflow,
        relax, flags, solid, swap, rows,
    )


def solution(mesh):
    placed = (
        P("mode", None, "space", None),
        P(None, "space"),
        P(None, "space"),
        P(),
        P("mode", None),
        P(),
        P(),
    )
    return jax.shard_map(
        on_device,
        mesh=mesh,
        in_specs=placed,
        out_specs=P("mode", None, "space", None),
        check_vma=False,
    )
```

```python
import math

import numpy as np
import jax
import jax.numpy as jnp
from jax import lax
from jax.experimental import pallas as pl
from jax.experimental.pallas import tpu as pltpu
from jax.sharding import PartitionSpec as P

VX = 24
V = 576
ROWS = 2
COLS = 16
OWN = 32
MODES = 16
K = 256
VMAX = 4.6
DT_DX = 0.09
RHO_FLOOR = 0.3
TEMP_FLOOR = 0.2
STEP = 2.0 * VMAX / (VX - 1)
WEIGHT = STEP * STEP
HALF = 0.5 * STEP
LOG2E = math.log2(math.e)

HALO = 32
FAR = 36
BOUNCE = 40
MIRROR = 76
EDGE = 112
INFLOW = 116
SLOTS = 117
GROUP = 16

F32 = jnp.float32
BF16 = jnp.bfloat16
NT = (((1,), (1,)), ((), ()))
CHUNKS = tuple((128 * j, min(128, V - 128 * j)) for j in range(5))
LIMIT = 56 * 1024 * 1024


def tables():
    index = np.arange(V)
    a, b = index // VX, index % VX
    odd_a, odd_b = 2 * a - (VX - 1), 2 * b - (VX - 1)
    tri = (odd_a * odd_a - 1) // 8 + (odd_b * odd_b - 1) // 8
    weights = np.stack([np.ones(V), odd_a, odd_b, tri], 1)
    weights = np.repeat(weights, 32, axis=1)
    turned = a * VX + (VX - 1 - b)
    swap = np.zeros((1152, 128), np.float32)
    lane = np.arange(128)
    swap[191 - lane, lane] = 1.0
    for at, left, out in ((256, 0, 0), (512, 0, 128), (896, 128, 256)):
        swap[at + turned[out + lane] - left, lane] = 1.0
    rows = np.zeros((8, V), np.float32)
    rows[0] = DT_DX * np.abs(-VMAX + STEP * a)
    rows[1] = DT_DX * np.abs(-VMAX + STEP * b)
    rows[2] = (a >= VX // 2).astype(np.float32)
    rows[3] = (b >= VX // 2).astype(np.float32)
    return (
        jnp.asarray(weights.astype(np.float32), BF16),
        jnp.asarray(swap, BF16),
        jnp.asarray(rows),
    )


def lanes(shape):
    return lax.broadcasted_iota(jnp.int32, shape, len(shape) - 1)


def pieces(value):
    hi = value.astype(BF16)
    rest = value - hi.astype(F32)
    mid = rest.astype(BF16)
    low = (rest - mid.astype(F32)).astype(BF16)
    return hi, mid, low


def cell_chunk(wide, cell, j):
    return wide[j, pl.ds(cell, MODES, stride=OWN), :]


def widen(dist, wide):
    for j, (at, n) in enumerate(CHUNKS):
        wide[j, :, :n] = dist[:, :, :, at : at + n].reshape(ROWS * COLS * MODES, n).astype(F32)


def edges_kernel(dist, relax, flags, to_left, to_right, wide):
    widen(dist, wide)
    lane = lanes((MODES, 128))
    for out, near, far, first in ((to_left, 0, 1, 0), (to_right, COLS - 1, COLS - 2, 2)):
        for r in range(ROWS):
            hi, mid, low = pieces(jnp.full((MODES, 128), relax[r, near], F32))
            flag = jnp.full((MODES, 128), flags[r, near], jnp.int32).astype(F32)
            extra = jnp.where(
                lane == 64,
                hi.astype(F32),
                jnp.where(
                    lane == 65,
                    mid.astype(F32),
                    jnp.where(lane == 66, low.astype(F32), jnp.where(lane == 67, flag, 0.0)),
                ),
            )
            for j in range(5):
                value = cell_chunk(wide, r * COLS + near, j)
                if j == 4:
                    value = jnp.where(lane < 64, value, extra)
                out[r * 8 + j] = value.astype(BF16)
            for j in range(3):
                value = cell_chunk(wide, r * COLS + far, first + j)
                if first + j == 4:
                    value = jnp.where(lane < 64, value, 0.0)
                out[r * 8 + 5 + j] = value.astype(BF16)


def turn(held, count, swap):
    parts = ((0, 256, 256, 128), (0, 384, 512, 128), (128, 256, 896, 128), (384, 192, 256, 128), (384, 192, 512, 64))
    return permuted(held, count, swap, parts)


def reverse(held, count, swap):
    parts = ((384, 192, 0, 128), (256, 256, 0, 128), (128, 256, 0, 128), (0, 256, 0, 128), (0, 128, 128, 64))
    return permuted(held, count, swap, parts)


def permuted(held, count, swap, parts):
    return [
        jnp.dot(held[:count, lane : lane + n], swap[at : at + n, :width], preferred_element_type=F32)
        for lane, n, at, width in parts
    ]


def mirrored(slots, held, cells, swap):
    rows = cells * MODES
    for (at, n), part in zip(CHUNKS, turn(held, rows, swap)):
        slots[MIRROR : MIRROR + cells, :, at : at + n] = part.reshape(cells, MODES, n)
        for e, cell in enumerate((0, COLS - 1, COLS, 2 * COLS - 1)):
            held[rows + e * MODES : rows + (e + 1) * MODES, at : at + n] = part[
                cell * MODES : (cell + 1) * MODES
            ].astype(BF16)
    for (at, n), part in zip(CHUNKS, reverse(held, rows + 64, swap)):
        slots[BOUNCE : BOUNCE + cells, :, at : at + n] = part[:rows].reshape(cells, MODES, n)
        slots[EDGE : EDGE + 4, :, at : at + n] = part[rows:].reshape(4, MODES, n)


def advection(slots, rows, h, left, right, below, above):
    up_x = jnp.where(rows[2:3, :] > 0.5, left, right)
    up_y = jnp.where(rows[3:4, :] > 0.5, below, above)
    return rows[0:1, :] * (up_x - h) + rows[1:2, :] * (up_y - h)


def sources(r, c, column, flags, solid):
    own = r * COLS + c
    flag = flags[r, c]
    bounced = BOUNCE + own
    last = COLS * 16 - 1
    left = jnp.where(c == 0, HALO + r * 2, own - 1)
    right = jnp.where(c == COLS - 1, HALO + r * 2 + 1, own + 1)
    solid_left = solid[r, jnp.maximum(column - 1, 0)] == 1
    solid_right = solid[r, jnp.minimum(column + 1, last)] == 1

    def edge(turned):
        return jnp.where(flag == 0, own, jnp.where(flag == 1, INFLOW, turned))

    left = jnp.where(column == 0, edge(EDGE + r * 2), jnp.where(solid_left, bounced, left))
    right = jnp.where(
        column == last, edge(EDGE + r * 2 + 1), jnp.where(solid_right, bounced, right)
    )
    outside = edge(MIRROR + own)
    other = (1 - r) * COLS + c
    inside = jnp.where(solid[1 - r, column] == 1, bounced, other)
    below, above = (outside, inside) if r == 0 else (inside, outside)
    return left, right, below, above


def fold(sums, count):
    place = lanes((MODES, 128)) % 32
    total = jnp.zeros((MODES, 128), F32)
    for i in range(count):
        total += jnp.where(place == i, sums[i * MODES : (i + 1) * MODES], 0.0)
    return total


def split(value, high, low, cell):
    hi = value.astype(BF16)
    at = pl.multiple_of(cell * MODES, MODES)
    high[pl.ds(at, MODES), :] = hi
    low[pl.ds(at, MODES), :] = (value - hi.astype(F32)).astype(BF16)


def explicit_kernel(
    dist, inflow, relax, flags, solid, weights, swap, rows,
    cells, ends, base, sums, wide, slots, held, high, low,
):
    first = lax.axis_index("space") * COLS
    widen(dist, wide)

    def gather(c, carry):
        for r in range(ROWS):
            cell = r * COLS + c
            at_held = pl.multiple_of(cell * MODES, MODES)
            for j, (at, n) in enumerate(CHUNKS):
                value = cell_chunk(wide, cell, j)[:, :n]
                slots[cell, :, at : at + n] = value
                held[pl.ds(at_held, MODES), at : at + n] = value.astype(BF16)
        return carry

    lax.fori_loop(0, COLS, gather, 0, unroll=2)
    cells[...] = held[: OWN * MODES, :].reshape(OWN, MODES, V)
    for e, cell in enumerate((0, COLS - 1, COLS, 2 * COLS - 1)):
        ends[e] = held[cell * MODES : (cell + 1) * MODES, :]
    slots[INFLOW] = inflow[...].astype(F32)
    slots[HALO : HALO + 4] = jnp.zeros((4, MODES, V), F32)
    mirrored(slots, held, OWN, swap)

    def own_cell(c, carry):
        for r in range(ROWS):
            cell = r * COLS + c
            column = first + c
            left, right, below, above = sources(r, c, column, flags, solid)
            h = slots[cell]
            moved = advection(
                slots, rows, h, slots[left], slots[right], slots[below], slots[above]
            )
            value = h - relax[r, c] * h + moved
            value = jnp.where(solid[r, column] == 0, value, 0.0)
            base[cell] = value
            split(value, high, low, cell)
        return carry

    lax.fori_loop(0, COLS, own_cell, 0, unroll=4)
    sums[0] = fold(
        jnp.dot(held[: OWN * MODES, :], weights[...], preferred_element_type=F32), OWN
    )
    sums[1] = fold(
        jnp.dot(high[...], weights[...], preferred_element_type=F32)
        + jnp.dot(low[...], weights[...], preferred_element_type=F32),
        OWN,
    )


def halo_kernel(
    from_left, from_right, ends, sums, inflow, solid, weights, swap, rows,
    pay, edge, rates, near, far, turned, back, held,
):
    first = lax.axis_index("space") * COLS
    last = COLS * 16 - 1
    for side, ref, start in ((0, from_left, 2), (1, from_right, 0)):
        for r in range(ROWS):
            i = r * 2 + side
            for j, (at, n) in enumerate(CHUNKS):
                value = ref[r * 8 + j][:, :n]
                near[i, :, at : at + n] = value.astype(F32)
                held[i * MODES : (i + 1) * MODES, at : at + n] = value
            for j in range(3):
                at, n = CHUNKS[start + j]
                far[i, :, at : at + n] = ref[r * 8 + 5 + j][:, :n].astype(F32)
    for (at, n), part in zip(CHUNKS, turn(held, 64, swap)):
        turned[:, :, at : at + n] = part.reshape(4, MODES, n)
    for (at, n), part in zip(CHUNKS, reverse(held, 64, swap)):
        back[:, :, at : at + n] = part.reshape(4, MODES, n)
    source = inflow[...].astype(F32)
    for side, ref in ((0, from_left), (1, from_right)):
        for r in range(ROWS):
            i = r * 2 + side
            beyond = first - 1 if side == 0 else first + COLS
            column = jnp.clip(beyond, 1, last - 1)
            extra = ref[r * 8 + 4].astype(F32)
            rate = extra[:, 64:65] + extra[:, 65:66] + extra[:, 66:67]
            flag = extra[:, 67:68]
            h = near[i]
            own = ends[i].astype(F32)
            bounced = back[i]
            left, right = (far[i], own) if side == 0 else (own, far[i])
            left = jnp.where(solid[r, column - 1] == 1, bounced, left)
            right = jnp.where(solid[r, column + 1] == 1, bounced, right)
            outside = jnp.where(flag < 0.5, h, jnp.where(flag < 1.5, source, turned[i]))
            inside = jnp.where(solid[1 - r, column] == 1, bounced, near[(1 - r) * 2 + side])
            below, above = (outside, inside) if r == 0 else (inside, outside)
            value = h - rate * h + advection(None, rows, h, left, right, below, above)
            fluid = solid[r, column] == 0
            edge[4 + i] = jnp.where(fluid, value, 0.0)
            rates[i] = jnp.broadcast_to(jnp.where(fluid, rate, 0.0), (MODES, 128))

            inner = first if side == 0 else first + COLS - 1
            inside_band = (beyond >= 0) & (beyond <= last)
            used = inside_band & (solid[r, jnp.clip(beyond, 0, last)] == 0) & (solid[r, inner] == 0)
            taken = rows[2:3, :] > 0.5 if side == 0 else rows[2:3, :] < 0.5
            value = jnp.where(taken, rows[0:1, :] * h, 0.0)
            value = jnp.where(used, value, 0.0)
            edge[i] = value
            hi = value.astype(BF16)
            held[64 + i * MODES : 80 + i * MODES, :] = hi
            held[128 + i * MODES : 144 + i * MODES, :] = (value - hi.astype(F32)).astype(BF16)
    edge[8] = jnp.zeros((MODES, V), F32)
    folded = jnp.dot(held[...], weights[...], preferred_element_type=F32)
    place = lanes((MODES, 128)) % 32
    added = folded[64:128] + folded[128:]
    later = sums[1]
    for i in range(4):
        cell = (i // 2) * COLS + (0 if i % 2 == 0 else COLS - 1)
        later += jnp.where(place == cell, added[i * MODES : (i + 1) * MODES], 0.0)
    row = lax.broadcasted_iota(jnp.int32, (64, 128), 0)
    lane = lanes((64, 128))
    chosen = ((lane % 32) // 4 == row % 8) & (lane % 4 == row // MODES)
    parts = jnp.where(chosen, folded[:64], 0.0)
    halves = []
    for half in (0, 8):
        total = sum(parts[i * MODES + half : i * MODES + half + 8] for i in range(4))
        halves.append(jnp.sum(total, 0, keepdims=True))
    ends_sums = jnp.concatenate(halves + [jnp.zeros((6, 128), F32)], 0)
    for d in range(16):
        pay[d, :16, :] = sums[0]
        pay[d, 16:32, :] = later
        pay[d, 32:40, :] = ends_sums


def exact_nt(value, table):
    total = None
    for piece in pieces(value):
        part = lax.dot_general(piece, table, NT, preferred_element_type=F32)
        total = part if total is None else total + part
    return total


def set_parameters(par, at, sums):
    s0, s1, s2, s3 = sums
    n = s0.shape[0]
    rho = WEIGHT * s0
    mx = (WEIGHT * HALF) * s1
    my = (WEIGHT * HALF) * s2
    en = (WEIGHT * HALF * HALF) * (4.0 * s3 + s0)
    safe = jnp.maximum(rho, RHO_FLOOR)
    ux = mx / safe
    uy = my / safe
    temp = jnp.maximum(en / safe - 0.5 * (ux * ux + uy * uy), TEMP_FLOOR)
    par[0, at : at + n] = ux
    par[1, at : at + n] = uy
    par[2, at : at + n] = (-0.5 * LOG2E) / temp
    par[3, at : at + n] = safe / (2.0 * math.pi * temp)


def factors(par, cell):
    ux = par[0, pl.ds(cell, 1), :]
    uy = par[1, pl.ds(cell, 1), :]
    rate = par[2, pl.ds(cell, 1), :]
    scale = par[3, pl.ds(cell, 1), :]
    speed = lax.broadcasted_iota(jnp.int32, (VX, K), 0).astype(F32) * STEP - VMAX
    dx = speed - ux
    dy = speed - uy
    return scale * jnp.exp2(dx * dx * rate), jnp.exp2(dy * dy * rate)


def project(along_x, along_y, equil, projection):
    for i in range(VX // 2):
        pair = jnp.concatenate(
            [along_x[2 * i : 2 * i + 1] * along_y, along_x[2 * i + 1 : 2 * i + 2] * along_y], 0
        )
        equil[48 * i : 48 * (i + 1), :] = pair.astype(BF16)
    out = lax.dot_general(projection, equil[...], NT, preferred_element_type=F32)
    return out.astype(BF16).astype(F32)


def collide_kernel(
    gathered, basis, projection, base_far, edge_far, cells_far, rates, inflow,
    relax, flags, solid, swap_far, rows,
    out, slots, held, par, sums1, equil, wide, base, edge, cells, swap, arrived,
):
    copies = [
        pltpu.make_async_copy(source, target, arrived.at[i])
        for i, (source, target) in enumerate(
            ((base_far, base), (edge_far, edge), (cells_far, cells), (swap_far, swap))
        )
    ]
    for copy in copies:
        copy.start()
    first = lax.axis_index("space") * COLS
    mode = lax.axis_index("mode") * MODES
    mine = projection[pl.ds(pl.multiple_of(mode, MODES), MODES), :]
    now = gathered[:, :16, :].reshape(K, 128).T
    later = gathered[:, 16:32, :].reshape(K, 128).T
    spread = jnp.broadcast_to(gathered[:, 32:34, :].reshape(32, 1, 128), (32, 8, 128)).reshape(K, 128)
    of_mode = lax.broadcasted_iota(jnp.int32, (K, 128), 0) % 8
    spread = jnp.where((lanes((K, 128)) % 32) // 4 == of_mode, spread, 0.0).T
    node = exact_nt(now, basis[...])
    halo_node = exact_nt(spread, basis[...])
    set_parameters(par, 0, [node[32 * i : 32 * i + 32] for i in range(4)])
    halo_sums = []
    for i in range(4):
        eight = sum(halo_node[32 * i + 8 * j : 32 * i + 8 * j + 8] for j in range(4))
        halo_sums.append(eight + jnp.concatenate([eight[4:], eight[:4]], 0))
    set_parameters(par, 32, halo_sums)
    slots[INFLOW] = inflow[...].astype(F32)

    odd = (2 * lax.broadcasted_iota(jnp.int32, (VX, K), 0) - (VX - 1)).astype(F32)
    tri = (odd * odd - 1.0) * 0.125

    def sums_of(value):
        return (
            jnp.sum(value, 0, keepdims=True),
            jnp.sum(value * odd, 0, keepdims=True),
            jnp.sum(value * tri, 0, keepdims=True),
        )

    def first_cell(c, slot):
        for r in range(ROWS):
            cell = r * COLS + c
            along_x, along_y = factors(par, cell)
            coll = project(along_x, along_y, equil.at[slot + r], mine)
            fluid = solid[r, first + c] == 0
            rate = jnp.where(fluid, relax[r, c], 0.0)
            end = jnp.where(c == 0, r * 2, jnp.where(c == COLS - 1, r * 2 + 1, 8))
            section = (base[cell] + edge[end] + rate * coll).astype(BF16)
            slots[cell] = section.astype(F32)
            held[pl.ds(pl.multiple_of(cell * MODES, MODES), MODES), :] = section
            x0, x1, x2 = sums_of(along_x)
            y0, y1, y2 = sums_of(along_y)
            y0, y1, y2 = rate * y0, rate * y1, rate * y2
            sums1[pl.ds(cell, 1), :] = x0 * y0
            sums1[pl.ds(32 + cell, 1), :] = x1 * y0
            sums1[pl.ds(64 + cell, 1), :] = x0 * y1
            sums1[pl.ds(96 + cell, 1), :] = x2 * y0 + x0 * y2

    def first_stage(i, carry):
        for u in range(GROUP):
            first_cell(i * GROUP + u, u * ROWS)
        return carry

    for copy in copies:
        copy.wait()
    lax.fori_loop(0, COLS // GROUP, first_stage, 0)
    for side in range(2):
        for r in range(ROWS):
            cell = HALO + r * 2 + side
            rate = rates[r * 2 + side][:, :1]
            along_x, along_y = factors(par, cell)
            coll = project(along_x, along_y, equil.at[r * 2 + side], mine)
            slots[cell] = (edge[4 + r * 2 + side] + rate * coll).astype(BF16).astype(F32)

    mirrored(slots, held, OWN, swap)
    mixed = later + exact_nt(sums1[...], projection[...])
    node = exact_nt(mixed, basis[...])
    set_parameters(par, 0, [node[32 * i : 32 * i + 32] for i in range(4)])

    def second_cell(c, slot):
        for r in range(ROWS):
            cell = r * COLS + c
            column = first + c
            along_x, along_y = factors(par, cell)
            coll = project(along_x, along_y, equil.at[slot + r], mine)
            left, right, below, above = sources(r, c, column, flags, solid)
            h = slots[cell]
            moved = advection(
                slots, rows, h, slots[left], slots[right], slots[below], slots[above]
            )
            value = h + moved + relax[r, c] * (coll - h)
            value = 0.5 * cells[cell].astype(F32) + 0.5 * value
            value = jnp.where(solid[r, column] == 0, value, 0.0)
            for j, (at, n) in enumerate(CHUNKS):
                wide[j, pl.ds(cell, MODES, stride=OWN), :n] = value[:, at : at + n]

    def second_stage(i, carry):
        for u in range(GROUP):
            second_cell(i * GROUP + u, u * ROWS)
        return carry

    lax.fori_loop(0, COLS // GROUP, second_stage, 0)
    for j, (at, n) in enumerate(CHUNKS):
        out[:, :, :, at : at + n] = (
            wide[j, :, :n].astype(BF16).reshape(MODES, ROWS, COLS, n)
        )


def on_device(dist, relax, flags, solid, inflow, basis, projection):
    weights, swap, rows = tables()
    vmem = pl.BlockSpec(memory_space=pltpu.VMEM)
    smem = pl.BlockSpec(memory_space=pltpu.SMEM)
    far = pl.BlockSpec(memory_space=pl.ANY)
    params = pltpu.CompilerParams(vmem_limit_bytes=LIMIT)

    to_left, to_right = pl.pallas_call(
        edges_kernel,
        out_shape=(
            jax.ShapeDtypeStruct((16, MODES, 128), BF16),
            jax.ShapeDtypeStruct((16, MODES, 128), BF16),
        ),
        in_specs=[vmem, smem, smem],
        out_specs=(vmem, vmem),
        scratch_shapes=[pltpu.VMEM((5, OWN * MODES, 128), F32)],
        compiler_params=params,
    )(dist, relax, flags)
    count = lax.axis_size("space")
    from_left = lax.ppermute(to_right, "space", [(i, (i + 1) % count) for i in range(count)])
    from_right = lax.ppermute(to_left, "space", [((i + 1) % count, i) for i in range(count)])

    cells, ends, base, sums = pl.pallas_call(
        explicit_kernel,
        out_shape=(
            jax.ShapeDtypeStruct((OWN, MODES, V), BF16),
            jax.ShapeDtypeStruct((4, MODES, V), BF16),
            jax.ShapeDtypeStruct((OWN, MODES, V), F32),
            jax.ShapeDtypeStruct((2, MODES, 128), F32),
        ),
        in_specs=[vmem] * 2 + [smem] * 3 + [vmem] * 3,
        out_specs=(vmem, vmem, vmem, vmem),
        scratch_shapes=[
            pltpu.VMEM((5, OWN * MODES, 128), F32),
            pltpu.VMEM((SLOTS, MODES, V), F32),
            pltpu.VMEM((576, V), BF16),
            pltpu.VMEM((OWN * MODES, V), BF16),
            pltpu.VMEM((OWN * MODES, V), BF16),
        ],
        compiler_params=params,
        cost_estimate=pl.CostEstimate(
            flops=20_000_000_000, bytes_accessed=4_000_000, transcendentals=0
        ),
    )(dist, inflow, relax, flags, solid, weights, swap, rows)

    pay, edge, rates = pl.pallas_call(
        halo_kernel,
        out_shape=(
            jax.ShapeDtypeStruct((16, 40, 128), F32),
            jax.ShapeDtypeStruct((9, MODES, V), F32),
            jax.ShapeDtypeStruct((4, MODES, 128), F32),
        ),
        in_specs=[vmem] * 5 + [smem] + [vmem] * 3,
        out_specs=(vmem, vmem, vmem),
        scratch_shapes=[pltpu.VMEM((4, MODES, V), F32)] * 4
        + [
            pltpu.VMEM((192, V), BF16),
        ],
        compiler_params=pltpu.CompilerParams(vmem_limit_bytes=63 * 1024 * 1024 + 900 * 1024),
    )(from_left, from_right, ends, sums, inflow, solid, weights, swap, rows)
    gathered = lax.all_to_all(pay, "mode", split_axis=0, concat_axis=0, tiled=True)

    return pl.pallas_call(
        collide_kernel,
        out_shape=jax.ShapeDtypeStruct((MODES, ROWS, COLS, V), BF16),
        in_specs=[vmem] * 3 + [far] * 3 + [vmem] * 2 + [smem] * 3 + [far, vmem],
        out_specs=vmem,
        scratch_shapes=[
            pltpu.VMEM((SLOTS, MODES, V), F32),
            pltpu.VMEM((576, V), BF16),
            pltpu.VMEM((4, 40, K), F32),
            pltpu.VMEM((128, K), F32),
            pltpu.VMEM((2 * GROUP, V, K), BF16),
            pltpu.VMEM((5, OWN * MODES, 128), F32),
            pltpu.VMEM((OWN, MODES, V), F32),
            pltpu.VMEM((9, MODES, V), F32),
            pltpu.VMEM((OWN, MODES, V), BF16),
            pltpu.VMEM((1152, 128), BF16),
            pltpu.SemaphoreType.DMA((4,)),
        ],
        compiler_params=params,
    )(
        gathered, basis, projection, base, edge, cells, rates, inflow,
        relax, flags, solid, swap, rows,
    )


def solution(mesh):
    placed = (
        P("mode", None, "space", None),
        P(None, "space"),
        P(None, "space"),
        P(),
        P("mode", None),
        P(),
        P(),
    )
    return jax.shard_map(
        on_device,
        mesh=mesh,
        in_specs=placed,
        out_specs=P("mode", None, "space", None),
        check_vma=False,
    )
```

```python
import math

import numpy as np
import jax
import jax.numpy as jnp
from jax import lax
from jax.experimental import pallas as pl
from jax.experimental.pallas import tpu as pltpu
from jax.sharding import PartitionSpec as P

VX = 24
V = 576
ROWS = 2
COLS = 16
OWN = 32
MODES = 16
K = 256
VMAX = 4.6
DT_DX = 0.09
RHO_FLOOR = 0.3
TEMP_FLOOR = 0.2
STEP = 2.0 * VMAX / (VX - 1)
WEIGHT = STEP * STEP
HALF = 0.5 * STEP
LOG2E = math.log2(math.e)

HALO = 32
FAR = 36
BOUNCE = 40
MIRROR = 76
EDGE = 112
INFLOW = 116
SLOTS = 117
GROUP = 16

F32 = jnp.float32
BF16 = jnp.bfloat16
NT = (((1,), (1,)), ((), ()))
CHUNKS = tuple((128 * j, min(128, V - 128 * j)) for j in range(5))
LIMIT = 56 * 1024 * 1024


def tables():
    index = np.arange(V)
    a, b = index // VX, index % VX
    odd_a, odd_b = 2 * a - (VX - 1), 2 * b - (VX - 1)
    tri = (odd_a * odd_a - 1) // 8 + (odd_b * odd_b - 1) // 8
    weights = np.stack([np.ones(V), odd_a, odd_b, tri], 1)
    weights = np.repeat(weights, 32, axis=1)
    turned = a * VX + (VX - 1 - b)
    swap = np.zeros((1152, 128), np.float32)
    lane = np.arange(128)
    swap[191 - lane, lane] = 1.0
    for at, left, out in ((256, 0, 0), (512, 0, 128), (896, 128, 256)):
        swap[at + turned[out + lane] - left, lane] = 1.0
    pair = np.arange(256)
    order = np.zeros((256, 256), np.float32)
    order[pair, pair % 16 * 16 + pair // 16] = 1.0
    rows = np.zeros((8, V), np.float32)
    rows[0] = DT_DX * np.abs(-VMAX + STEP * a)
    rows[1] = DT_DX * np.abs(-VMAX + STEP * b)
    rows[2] = (a >= VX // 2).astype(np.float32)
    rows[3] = (b >= VX // 2).astype(np.float32)
    return (
        jnp.asarray(weights.astype(np.float32), BF16),
        jnp.asarray(swap, BF16),
        jnp.asarray(rows),
        jnp.asarray(order, BF16),
    )


def lanes(shape):
    return lax.broadcasted_iota(jnp.int32, shape, len(shape) - 1)


def pieces(value):
    hi = value.astype(BF16)
    rest = value - hi.astype(F32)
    mid = rest.astype(BF16)
    low = (rest - mid.astype(F32)).astype(BF16)
    return hi, mid, low


def cell_chunk(wide, cell, j):
    return wide[j, pl.ds(cell, MODES, stride=OWN), :]


def widen(dist, wide):
    for j, (at, n) in enumerate(CHUNKS):
        wide[j, :, :n] = dist[:, :, :, at : at + n].reshape(ROWS * COLS * MODES, n).astype(F32)


def edges_kernel(dist, relax, flags, to_left, to_right, wide):
    widen(dist, wide)
    lane = lanes((MODES, 128))
    for out, near, far, first in ((to_left, 0, 1, 0), (to_right, COLS - 1, COLS - 2, 2)):
        for r in range(ROWS):
            hi, mid, low = pieces(jnp.full((MODES, 128), relax[r, near], F32))
            flag = jnp.full((MODES, 128), flags[r, near], jnp.int32).astype(F32)
            extra = jnp.where(
                lane == 64,
                hi.astype(F32),
                jnp.where(
                    lane == 65,
                    mid.astype(F32),
                    jnp.where(lane == 66, low.astype(F32), jnp.where(lane == 67, flag, 0.0)),
                ),
            )
            for j in range(5):
                value = cell_chunk(wide, r * COLS + near, j)
                if j == 4:
                    value = jnp.where(lane < 64, value, extra)
                out[r * 8 + j] = value.astype(BF16)
            for j in range(3):
                value = cell_chunk(wide, r * COLS + far, first + j)
                if first + j == 4:
                    value = jnp.where(lane < 64, value, 0.0)
                out[r * 8 + 5 + j] = value.astype(BF16)


def turn(held, count, swap):
    parts = ((0, 256, 256, 128), (0, 384, 512, 128), (128, 256, 896, 128), (384, 192, 256, 128), (384, 192, 512, 64))
    return permuted(held, count, swap, parts)


def reverse(held, count, swap):
    parts = ((384, 192, 0, 128), (256, 256, 0, 128), (128, 256, 0, 128), (0, 256, 0, 128), (0, 128, 128, 64))
    return permuted(held, count, swap, parts)


def permuted(held, count, swap, parts):
    return [
        jnp.dot(held[:count, lane : lane + n], swap[at : at + n, :width], preferred_element_type=F32)
        for lane, n, at, width in parts
    ]


def mirrored(slots, held, cells, swap):
    rows = cells * MODES
    for (at, n), part in zip(CHUNKS, turn(held, rows, swap)):
        slots[MIRROR : MIRROR + cells, :, at : at + n] = part.reshape(cells, MODES, n)
        for e, cell in enumerate((0, COLS - 1, COLS, 2 * COLS - 1)):
            held[rows + e * MODES : rows + (e + 1) * MODES, at : at + n] = part[
                cell * MODES : (cell + 1) * MODES
            ].astype(BF16)
    for (at, n), part in zip(CHUNKS, reverse(held, rows + 64, swap)):
        slots[BOUNCE : BOUNCE + cells, :, at : at + n] = part[:rows].reshape(cells, MODES, n)
        slots[EDGE : EDGE + 4, :, at : at + n] = part[rows:].reshape(4, MODES, n)


def advection(slots, rows, h, left, right, below, above):
    up_x = jnp.where(rows[2:3, :] > 0.5, left, right)
    up_y = jnp.where(rows[3:4, :] > 0.5, below, above)
    return rows[0:1, :] * (up_x - h) + rows[1:2, :] * (up_y - h)


def sources(r, c, column, flags, solid):
    own = r * COLS + c
    flag = flags[r, c]
    bounced = BOUNCE + own
    last = COLS * 16 - 1
    left = jnp.where(c == 0, HALO + r * 2, own - 1)
    right = jnp.where(c == COLS - 1, HALO + r * 2 + 1, own + 1)
    solid_left = solid[r, jnp.maximum(column - 1, 0)] == 1
    solid_right = solid[r, jnp.minimum(column + 1, last)] == 1

    def edge(turned):
        return jnp.where(flag == 0, own, jnp.where(flag == 1, INFLOW, turned))

    left = jnp.where(column == 0, edge(EDGE + r * 2), jnp.where(solid_left, bounced, left))
    right = jnp.where(
        column == last, edge(EDGE + r * 2 + 1), jnp.where(solid_right, bounced, right)
    )
    outside = edge(MIRROR + own)
    other = (1 - r) * COLS + c
    inside = jnp.where(solid[1 - r, column] == 1, bounced, other)
    below, above = (outside, inside) if r == 0 else (inside, outside)
    return left, right, below, above


def fold(sums, count):
    place = lanes((MODES, 128)) % 32
    total = jnp.zeros((MODES, 128), F32)
    for i in range(count):
        total += jnp.where(place == i, sums[i * MODES : (i + 1) * MODES], 0.0)
    return total


def split(value, high, low, cell):
    hi = value.astype(BF16)
    at = pl.multiple_of(cell * MODES, MODES)
    high[pl.ds(at, MODES), :] = hi
    low[pl.ds(at, MODES), :] = (value - hi.astype(F32)).astype(BF16)


def by_other(value, order):
    return jnp.dot(order[...], value, preferred_element_type=F32)


def explicit_kernel(
    dist, inflow, relax, flags, solid, weights, swap, rows, order,
    cells, ends, base, sums, slots, held, high, low,
):
    first = lax.axis_index("space") * COLS
    for r in range(ROWS):
        top = r * COLS
        value = by_other(dist[:, r, :, :].reshape(COLS * MODES, V), order)
        slots[top : top + COLS] = value.reshape(COLS, MODES, V)
        held[top * MODES : (top + COLS) * MODES, :] = value.astype(BF16)
    cells[...] = held[: OWN * MODES, :]
    for e, cell in enumerate((0, COLS - 1, COLS, 2 * COLS - 1)):
        ends[e] = held[cell * MODES : (cell + 1) * MODES, :]
    slots[INFLOW] = inflow[...].astype(F32)
    slots[HALO : HALO + 4] = jnp.zeros((4, MODES, V), F32)
    mirrored(slots, held, OWN, swap)

    def own_cell(c, carry):
        for r in range(ROWS):
            cell = r * COLS + c
            column = first + c
            left, right, below, above = sources(r, c, column, flags, solid)
            h = slots[cell]
            moved = advection(
                slots, rows, h, slots[left], slots[right], slots[below], slots[above]
            )
            value = h - relax[r, c] * h + moved
            value = jnp.where(solid[r, column] == 0, value, 0.0)
            base[cell] = value
            split(value, high, low, cell)
        return carry

    lax.fori_loop(0, COLS, own_cell, 0, unroll=4)
    sums[0] = fold(
        jnp.dot(held[: OWN * MODES, :], weights[...], preferred_element_type=F32), OWN
    )
    sums[1] = fold(
        jnp.dot(high[...], weights[...], preferred_element_type=F32)
        + jnp.dot(low[...], weights[...], preferred_element_type=F32),
        OWN,
    )


def halo_kernel(
    from_left, from_right, ends, sums, inflow, solid, weights, swap, rows,
    pay, edge, rates, near, far, turned, back, held,
):
    first = lax.axis_index("space") * COLS
    last = COLS * 16 - 1
    for side, ref, start in ((0, from_left, 2), (1, from_right, 0)):
        for r in range(ROWS):
            i = r * 2 + side
            for j, (at, n) in enumerate(CHUNKS):
                value = ref[r * 8 + j][:, :n]
                near[i, :, at : at + n] = value.astype(F32)
                held[i * MODES : (i + 1) * MODES, at : at + n] = value
            for j in range(3):
                at, n = CHUNKS[start + j]
                far[i, :, at : at + n] = ref[r * 8 + 5 + j][:, :n].astype(F32)
    for (at, n), part in zip(CHUNKS, turn(held, 64, swap)):
        turned[:, :, at : at + n] = part.reshape(4, MODES, n)
    for (at, n), part in zip(CHUNKS, reverse(held, 64, swap)):
        back[:, :, at : at + n] = part.reshape(4, MODES, n)
    source = inflow[...].astype(F32)
    for side, ref in ((0, from_left), (1, from_right)):
        for r in range(ROWS):
            i = r * 2 + side
            beyond = first - 1 if side == 0 else first + COLS
            column = jnp.clip(beyond, 1, last - 1)
            extra = ref[r * 8 + 4].astype(F32)
            rate = extra[:, 64:65] + extra[:, 65:66] + extra[:, 66:67]
            flag = extra[:, 67:68]
            h = near[i]
            own = ends[i].astype(F32)
            bounced = back[i]
            left, right = (far[i], own) if side == 0 else (own, far[i])
            left = jnp.where(solid[r, column - 1] == 1, bounced, left)
            right = jnp.where(solid[r, column + 1] == 1, bounced, right)
            outside = jnp.where(flag < 0.5, h, jnp.where(flag < 1.5, source, turned[i]))
            inside = jnp.where(solid[1 - r, column] == 1, bounced, near[(1 - r) * 2 + side])
            below, above = (outside, inside) if r == 0 else (inside, outside)
            value = h - rate * h + advection(None, rows, h, left, right, below, above)
            fluid = solid[r, column] == 0
            edge[4 + i] = jnp.where(fluid, value, 0.0)
            rates[i] = jnp.broadcast_to(jnp.where(fluid, rate, 0.0), (MODES, 128))

            inner = first if side == 0 else first + COLS - 1
            inside_band = (beyond >= 0) & (beyond <= last)
            used = inside_band & (solid[r, jnp.clip(beyond, 0, last)] == 0) & (solid[r, inner] == 0)
            taken = rows[2:3, :] > 0.5 if side == 0 else rows[2:3, :] < 0.5
            value = jnp.where(taken, rows[0:1, :] * h, 0.0)
            value = jnp.where(used, value, 0.0)
            edge[i] = value
            hi = value.astype(BF16)
            held[64 + i * MODES : 80 + i * MODES, :] = hi
            held[128 + i * MODES : 144 + i * MODES, :] = (value - hi.astype(F32)).astype(BF16)
    edge[8] = jnp.zeros((MODES, V), F32)
    folded = jnp.dot(held[...], weights[...], preferred_element_type=F32)
    place = lanes((MODES, 128)) % 32
    added = folded[64:128] + folded[128:]
    later = sums[1]
    for i in range(4):
        cell = (i // 2) * COLS + (0 if i % 2 == 0 else COLS - 1)
        later += jnp.where(place == cell, added[i * MODES : (i + 1) * MODES], 0.0)
    row = lax.broadcasted_iota(jnp.int32, (64, 128), 0)
    lane = lanes((64, 128))
    chosen = ((lane % 32) // 4 == row % 8) & (lane % 4 == row // MODES)
    parts = jnp.where(chosen, folded[:64], 0.0)
    halves = []
    for half in (0, 8):
        total = sum(parts[i * MODES + half : i * MODES + half + 8] for i in range(4))
        halves.append(jnp.sum(total, 0, keepdims=True))
    ends_sums = jnp.concatenate(halves + [jnp.zeros((6, 128), F32)], 0)
    for d in range(16):
        pay[d, :16, :] = sums[0]
        pay[d, 16:32, :] = later
        pay[d, 32:40, :] = ends_sums


def exact_nt(value, table):
    total = None
    for piece in pieces(value)[:2]:
        part = lax.dot_general(piece, table, NT, preferred_element_type=F32)
        total = part if total is None else total + part
    return total


def set_parameters(par, at, sums):
    s0, s1, s2, s3 = sums
    n = s0.shape[0]
    rho = WEIGHT * s0
    mx = (WEIGHT * HALF) * s1
    my = (WEIGHT * HALF) * s2
    en = (WEIGHT * HALF * HALF) * (4.0 * s3 + s0)
    safe = jnp.maximum(rho, RHO_FLOOR)
    ux = mx / safe
    uy = my / safe
    temp = jnp.maximum(en / safe - 0.5 * (ux * ux + uy * uy), TEMP_FLOOR)
    par[0, at : at + n] = ux
    par[1, at : at + n] = uy
    par[2, at : at + n] = (-0.5 * LOG2E) / temp
    par[3, at : at + n] = safe / (2.0 * math.pi * temp)


def factors(par, cell):
    ux = par[0, pl.ds(cell, 1), :]
    uy = par[1, pl.ds(cell, 1), :]
    rate = par[2, pl.ds(cell, 1), :]
    scale = par[3, pl.ds(cell, 1), :]
    speed = lax.broadcasted_iota(jnp.int32, (VX, K), 0).astype(F32) * STEP - VMAX
    dx = speed - ux
    dy = speed - uy
    return scale * jnp.exp2(dx * dx * rate), jnp.exp2(dy * dy * rate)


def project(along_x, along_y, equil, projection):
    for i in range(VX // 2):
        pair = jnp.concatenate(
            [along_x[2 * i : 2 * i + 1] * along_y, along_x[2 * i + 1 : 2 * i + 2] * along_y], 0
        )
        equil[48 * i : 48 * (i + 1), :] = pair.astype(BF16)
    out = lax.dot_general(projection, equil[...], NT, preferred_element_type=F32)
    return out.astype(BF16).astype(F32)


def collide_kernel(
    gathered, basis, projection, base_far, edge_far, cells_far, rates, inflow,
    relax, flags, solid, swap_far, rows, order,
    out, slots, held, par, sums1, equil, base, edge, cells, swap, arrived, ready, written,
):
    copies = [
        pltpu.make_async_copy(source, target, arrived.at[i])
        for i, (source, target) in enumerate(
            ((base_far, base), (edge_far, edge), (cells_far, cells), (swap_far, swap))
        )
    ]
    for copy in copies:
        copy.start()
    first = lax.axis_index("space") * COLS
    mode = lax.axis_index("mode") * MODES
    mine = projection[pl.ds(pl.multiple_of(mode, MODES), MODES), :]
    now = gathered[:, :16, :].reshape(K, 128).T
    later = gathered[:, 16:32, :].reshape(K, 128).T
    spread = jnp.broadcast_to(gathered[:, 32:34, :].reshape(32, 1, 128), (32, 8, 128)).reshape(K, 128)
    of_mode = lax.broadcasted_iota(jnp.int32, (K, 128), 0) % 8
    spread = jnp.where((lanes((K, 128)) % 32) // 4 == of_mode, spread, 0.0).T
    node = exact_nt(now, basis[...])
    halo_node = exact_nt(spread, basis[...])
    set_parameters(par, 0, [node[32 * i : 32 * i + 32] for i in range(4)])
    halo_sums = []
    for i in range(4):
        eight = sum(halo_node[32 * i + 8 * j : 32 * i + 8 * j + 8] for j in range(4))
        halo_sums.append(eight + jnp.concatenate([eight[4:], eight[:4]], 0))
    set_parameters(par, 32, halo_sums)
    slots[INFLOW] = inflow[...].astype(F32)

    odd = (2 * lax.broadcasted_iota(jnp.int32, (VX, K), 0) - (VX - 1)).astype(F32)
    tri = (odd * odd - 1.0) * 0.125

    def sums_of(value):
        return (
            jnp.sum(value, 0, keepdims=True),
            jnp.sum(value * odd, 0, keepdims=True),
            jnp.sum(value * tri, 0, keepdims=True),
        )

    def first_cell(c, slot):
        for r in range(ROWS):
            cell = r * COLS + c
            along_x, along_y = factors(par, cell)
            coll = project(along_x, along_y, equil.at[slot + r], mine)
            fluid = solid[r, first + c] == 0
            rate = jnp.where(fluid, relax[r, c], 0.0)
            end = jnp.where(c == 0, r * 2, jnp.where(c == COLS - 1, r * 2 + 1, 8))
            section = (base[cell] + edge[end] + rate * coll).astype(BF16)
            slots[cell] = section.astype(F32)
            held[pl.ds(pl.multiple_of(cell * MODES, MODES), MODES), :] = section
            x0, x1, x2 = sums_of(along_x)
            y0, y1, y2 = sums_of(along_y)
            y0, y1, y2 = rate * y0, rate * y1, rate * y2
            sums1[pl.ds(cell, 1), :] = x0 * y0
            sums1[pl.ds(32 + cell, 1), :] = x1 * y0
            sums1[pl.ds(64 + cell, 1), :] = x0 * y1
            sums1[pl.ds(96 + cell, 1), :] = x2 * y0 + x0 * y2

    def first_stage(i, carry):
        for u in range(GROUP):
            first_cell(i * GROUP + u, u * ROWS)
        return carry

    for copy in copies:
        copy.wait()
    lax.fori_loop(0, COLS // GROUP, first_stage, 0)
    for side in range(2):
        for r in range(ROWS):
            cell = HALO + r * 2 + side
            rate = rates[r * 2 + side][:, :1]
            along_x, along_y = factors(par, cell)
            coll = project(along_x, along_y, equil.at[r * 2 + side], mine)
            slots[cell] = (edge[4 + r * 2 + side] + rate * coll).astype(BF16).astype(F32)

    mirrored(slots, held, OWN, swap)
    mixed = later + exact_nt(sums1[...], projection[...])
    node = exact_nt(mixed, basis[...])
    set_parameters(par, 0, [node[32 * i : 32 * i + 32] for i in range(4)])

    writes = []
    for r in range(ROWS):
        for c in range(COLS):
            cell = r * COLS + c
            column = first + c
            along_x, along_y = factors(par, cell)
            coll = project(along_x, along_y, equil.at[cell], mine)
            left, right, below, above = sources(r, c, column, flags, solid)
            h = slots[cell]
            moved = advection(
                slots, rows, h, slots[left], slots[right], slots[below], slots[above]
            )
            value = h + moved + relax[r, c] * (coll - h)
            before = cells[cell * MODES : (cell + 1) * MODES, :].astype(F32)
            value = 0.5 * before + 0.5 * value
            value = jnp.where(solid[r, column] == 0, value, 0.0)
            held[cell * MODES : (cell + 1) * MODES, :] = value.astype(BF16)
        top = r * COLS * MODES
        value = by_other(held[top : top + COLS * MODES, :], order)
        ready[:, r, :, :] = value.astype(BF16).reshape(MODES, COLS, V)
        write = pltpu.make_async_copy(ready.at[:, r], out.at[:, r], written.at[r])
        write.start()
        writes.append(write)
    for write in writes:
        write.wait()


def on_device(dist, relax, flags, solid, inflow, basis, projection):
    weights, swap, rows, order = tables()
    vmem = pl.BlockSpec(memory_space=pltpu.VMEM)
    smem = pl.BlockSpec(memory_space=pltpu.SMEM)
    far = pl.BlockSpec(memory_space=pl.ANY)
    params = pltpu.CompilerParams(vmem_limit_bytes=LIMIT)

    to_left, to_right = pl.pallas_call(
        edges_kernel,
        out_shape=(
            jax.ShapeDtypeStruct((16, MODES, 128), BF16),
            jax.ShapeDtypeStruct((16, MODES, 128), BF16),
        ),
        in_specs=[vmem, smem, smem],
        out_specs=(vmem, vmem),
        scratch_shapes=[pltpu.VMEM((5, OWN * MODES, 128), F32)],
        compiler_params=params,
    )(dist, relax, flags)
    count = lax.axis_size("space")
    from_left = lax.ppermute(to_right, "space", [(i, (i + 1) % count) for i in range(count)])
    from_right = lax.ppermute(to_left, "space", [((i + 1) % count, i) for i in range(count)])

    cells, ends, base, sums = pl.pallas_call(
        explicit_kernel,
        out_shape=(
            jax.ShapeDtypeStruct((OWN * MODES, V), BF16),
            jax.ShapeDtypeStruct((4, MODES, V), BF16),
            jax.ShapeDtypeStruct((OWN, MODES, V), F32),
            jax.ShapeDtypeStruct((2, MODES, 128), F32),
        ),
        in_specs=[vmem] * 2 + [smem] * 3 + [vmem] * 4,
        out_specs=(vmem, vmem, vmem, vmem),
        scratch_shapes=[
            pltpu.VMEM((SLOTS, MODES, V), F32),
            pltpu.VMEM((576, V), BF16),
            pltpu.VMEM((OWN * MODES, V), BF16),
            pltpu.VMEM((OWN * MODES, V), BF16),
        ],
        compiler_params=params,
        cost_estimate=pl.CostEstimate(
            flops=20_000_000_000, bytes_accessed=4_000_000, transcendentals=0
        ),
    )(dist, inflow, relax, flags, solid, weights, swap, rows, order)

    pay, edge, rates = pl.pallas_call(
        halo_kernel,
        out_shape=(
            jax.ShapeDtypeStruct((16, 40, 128), F32),
            jax.ShapeDtypeStruct((9, MODES, V), F32),
            jax.ShapeDtypeStruct((4, MODES, 128), F32),
        ),
        in_specs=[vmem] * 5 + [smem] + [vmem] * 3,
        out_specs=(vmem, vmem, vmem),
        scratch_shapes=[pltpu.VMEM((4, MODES, V), F32)] * 4
        + [
            pltpu.VMEM((192, V), BF16),
        ],
        compiler_params=pltpu.CompilerParams(vmem_limit_bytes=63 * 1024 * 1024 + 900 * 1024),
    )(from_left, from_right, ends, sums, inflow, solid, weights, swap, rows)
    gathered = lax.all_to_all(pay, "mode", split_axis=0, concat_axis=0, tiled=True)

    return pl.pallas_call(
        collide_kernel,
        out_shape=jax.ShapeDtypeStruct((MODES, ROWS, COLS, V), BF16),
        in_specs=[vmem] * 3 + [far] * 3 + [vmem] * 2 + [smem] * 3 + [far, vmem, vmem],
        out_specs=far,
        scratch_shapes=[
            pltpu.VMEM((SLOTS, MODES, V), F32),
            pltpu.VMEM((576, V), BF16),
            pltpu.VMEM((4, 40, K), F32),
            pltpu.VMEM((128, K), F32),
            pltpu.VMEM((2 * GROUP, V, K), BF16),
            pltpu.VMEM((OWN, MODES, V), F32),
            pltpu.VMEM((9, MODES, V), F32),
            pltpu.VMEM((OWN * MODES, V), BF16),
            pltpu.VMEM((1152, 128), BF16),
            pltpu.SemaphoreType.DMA((4,)),
            pltpu.VMEM((MODES, ROWS, COLS, V), BF16),
            pltpu.SemaphoreType.DMA((ROWS,)),
        ],
        compiler_params=params,
    )(
        gathered, basis, projection, base, edge, cells, rates, inflow,
        relax, flags, solid, swap, rows, order,
    )


def solution(mesh):
    placed = (
        P("mode", None, "space", None),
        P(None, "space"),
        P(None, "space"),
        P(),
        P("mode", None),
        P(),
        P(),
    )
    return jax.shard_map(
        on_device,
        mesh=mesh,
        in_specs=placed,
        out_specs=P("mode", None, "space", None),
        check_vma=False,
    )
```

```python
import math

import numpy as np
import jax
import jax.numpy as jnp
from jax import lax
from jax.experimental import pallas as pl
from jax.experimental.pallas import tpu as pltpu
from jax.sharding import PartitionSpec as P

VX = 24
V = 576
ROWS = 2
COLS = 16
OWN = 32
MODES = 16
K = 256
VMAX = 4.6
DT_DX = 0.09
RHO_FLOOR = 0.3
TEMP_FLOOR = 0.2
STEP = 2.0 * VMAX / (VX - 1)
WEIGHT = STEP * STEP
HALF = 0.5 * STEP
LOG2E = math.log2(math.e)

HALO = 32
FAR = 36
BOUNCE = 40
MIRROR = 76
EDGE = 112
INFLOW = 116
SLOTS = 117
GROUP = 16

F32 = jnp.float32
BF16 = jnp.bfloat16
NT = (((1,), (1,)), ((), ()))
CHUNKS = tuple((128 * j, min(128, V - 128 * j)) for j in range(5))
LIMIT = 56 * 1024 * 1024


def tables():
    index = np.arange(V)
    a, b = index // VX, index % VX
    odd_a, odd_b = 2 * a - (VX - 1), 2 * b - (VX - 1)
    tri = (odd_a * odd_a - 1) // 8 + (odd_b * odd_b - 1) // 8
    weights = np.stack([np.ones(V), odd_a, odd_b, tri], 1)
    weights = np.repeat(weights, 32, axis=1)
    turned = a * VX + (VX - 1 - b)
    swap = np.zeros((1152, 128), np.float32)
    lane = np.arange(128)
    swap[191 - lane, lane] = 1.0
    for at, left, out in ((256, 0, 0), (512, 0, 128), (896, 128, 256)):
        swap[at + turned[out + lane] - left, lane] = 1.0
    pair = np.arange(256)
    order = np.zeros((256, 256), np.float32)
    order[pair, pair % 16 * 16 + pair // 16] = 1.0
    rows = np.zeros((8, V), np.float32)
    rows[0] = DT_DX * np.abs(-VMAX + STEP * a)
    rows[1] = DT_DX * np.abs(-VMAX + STEP * b)
    rows[2] = (a >= VX // 2).astype(np.float32)
    rows[3] = (b >= VX // 2).astype(np.float32)
    return (
        jnp.asarray(weights.astype(np.float32), BF16),
        jnp.asarray(swap, BF16),
        jnp.asarray(rows),
        jnp.asarray(order, BF16),
        jnp.asarray(np.concatenate([order[:32], order[224:]]), BF16),
    )


def lanes(shape):
    return lax.broadcasted_iota(jnp.int32, shape, len(shape) - 1)


def pieces(value):
    hi = value.astype(BF16)
    rest = value - hi.astype(F32)
    mid = rest.astype(BF16)
    low = (rest - mid.astype(F32)).astype(BF16)
    return hi, mid, low


def edges_kernel(dist, relax, flags, pick, to_left, to_right):
    lane = lanes((MODES, 128))
    for r in range(ROWS):
        taken = by_other(dist[:, r, :, :].reshape(COLS * MODES, V), pick)
        for out, near, at_near, at_far, first in (
            (to_left, 0, 0, 1, 0),
            (to_right, COLS - 1, 3, 2, 2),
        ):
            hi, mid, low = pieces(jnp.full((MODES, 128), relax[r, near], F32))
            flag = jnp.full((MODES, 128), flags[r, near], jnp.int32).astype(F32)
            extra = jnp.where(
                lane == 64,
                hi.astype(F32),
                jnp.where(
                    lane == 65,
                    mid.astype(F32),
                    jnp.where(lane == 66, low.astype(F32), jnp.where(lane == 67, flag, 0.0)),
                ),
            )
            for j, (at, n) in enumerate(CHUNKS):
                value = taken[at_near * MODES : (at_near + 1) * MODES, at : at + n]
                if j == 4:
                    value = jnp.concatenate([value, extra[:, n:]], 1)
                out[r * 8 + j] = value.astype(BF16)
            for j in range(3):
                at, n = CHUNKS[first + j]
                value = taken[at_far * MODES : (at_far + 1) * MODES, at : at + n]
                if n < 128:
                    value = jnp.concatenate([value, jnp.zeros((MODES, 128 - n), F32)], 1)
                out[r * 8 + 5 + j] = value.astype(BF16)


def turn(held, count, swap):
    parts = ((0, 256, 256, 128), (0, 384, 512, 128), (128, 256, 896, 128), (384, 192, 256, 128), (384, 192, 512, 64))
    return permuted(held, count, swap, parts)


def reverse(held, count, swap):
    parts = ((384, 192, 0, 128), (256, 256, 0, 128), (128, 256, 0, 128), (0, 256, 0, 128), (0, 128, 128, 64))
    return permuted(held, count, swap, parts)


def permuted(held, count, swap, parts):
    return [
        jnp.dot(held[:count, lane : lane + n], swap[at : at + n, :width], preferred_element_type=F32)
        for lane, n, at, width in parts
    ]


def mirrored(slots, held, cells, swap):
    rows = cells * MODES
    for (at, n), part in zip(CHUNKS, turn(held, rows, swap)):
        slots[MIRROR : MIRROR + cells, :, at : at + n] = part.reshape(cells, MODES, n)
        for e, cell in enumerate((0, COLS - 1, COLS, 2 * COLS - 1)):
            held[rows + e * MODES : rows + (e + 1) * MODES, at : at + n] = part[
                cell * MODES : (cell + 1) * MODES
            ].astype(BF16)
    for (at, n), part in zip(CHUNKS, reverse(held, rows + 64, swap)):
        slots[BOUNCE : BOUNCE + cells, :, at : at + n] = part[:rows].reshape(cells, MODES, n)
        slots[EDGE : EDGE + 4, :, at : at + n] = part[rows:].reshape(4, MODES, n)


def advection(slots, rows, h, left, right, below, above):
    up_x = jnp.where(rows[2:3, :] > 0.5, left, right)
    up_y = jnp.where(rows[3:4, :] > 0.5, below, above)
    return rows[0:1, :] * (up_x - h) + rows[1:2, :] * (up_y - h)


def sources(r, c, column, flags, solid):
    own = r * COLS + c
    flag = flags[r, c]
    bounced = BOUNCE + own
    last = COLS * 16 - 1
    left = jnp.where(c == 0, HALO + r * 2, own - 1)
    right = jnp.where(c == COLS - 1, HALO + r * 2 + 1, own + 1)
    solid_left = solid[r, jnp.maximum(column - 1, 0)] == 1
    solid_right = solid[r, jnp.minimum(column + 1, last)] == 1

    def edge(turned):
        return jnp.where(flag == 0, own, jnp.where(flag == 1, INFLOW, turned))

    left = jnp.where(column == 0, edge(EDGE + r * 2), jnp.where(solid_left, bounced, left))
    right = jnp.where(
        column == last, edge(EDGE + r * 2 + 1), jnp.where(solid_right, bounced, right)
    )
    outside = edge(MIRROR + own)
    other = (1 - r) * COLS + c
    inside = jnp.where(solid[1 - r, column] == 1, bounced, other)
    below, above = (outside, inside) if r == 0 else (inside, outside)
    return left, right, below, above


def fold(sums, count):
    place = lanes((MODES, 128)) % 32
    total = jnp.zeros((MODES, 128), F32)
    for i in range(count):
        total += jnp.where(place == i, sums[i * MODES : (i + 1) * MODES], 0.0)
    return total


def split(value, high, low, cell):
    hi = value.astype(BF16)
    at = pl.multiple_of(cell * MODES, MODES)
    high[pl.ds(at, MODES), :] = hi
    low[pl.ds(at, MODES), :] = (value - hi.astype(F32)).astype(BF16)


def by_other(value, order):
    return jnp.dot(order[...], value, preferred_element_type=F32)


def explicit_kernel(
    dist, inflow, relax, flags, solid, weights, swap, rows, order,
    cells, ends, base, sums, slots, held, high, low,
):
    first = lax.axis_index("space") * COLS
    for r in range(ROWS):
        top = r * COLS
        value = by_other(dist[:, r, :, :].reshape(COLS * MODES, V), order)
        slots[top : top + COLS] = value.reshape(COLS, MODES, V)
        held[top * MODES : (top + COLS) * MODES, :] = value.astype(BF16)
    cells[...] = held[: OWN * MODES, :]
    for e, cell in enumerate((0, COLS - 1, COLS, 2 * COLS - 1)):
        ends[e] = held[cell * MODES : (cell + 1) * MODES, :]
    slots[INFLOW] = inflow[...].astype(F32)
    slots[HALO : HALO + 4] = jnp.zeros((4, MODES, V), F32)
    mirrored(slots, held, OWN, swap)

    def own_cell(c, carry):
        for r in range(ROWS):
            cell = r * COLS + c
            column = first + c
            left, right, below, above = sources(r, c, column, flags, solid)
            h = slots[cell]
            moved = advection(
                slots, rows, h, slots[left], slots[right], slots[below], slots[above]
            )
            value = h - relax[r, c] * h + moved
            value = jnp.where(solid[r, column] == 0, value, 0.0)
            base[cell] = value
            split(value, high, low, cell)
        return carry

    lax.fori_loop(0, COLS, own_cell, 0, unroll=4)
    sums[0] = fold(
        jnp.dot(held[: OWN * MODES, :], weights[...], preferred_element_type=F32), OWN
    )
    sums[1] = fold(
        jnp.dot(high[...], weights[...], preferred_element_type=F32)
        + jnp.dot(low[...], weights[...], preferred_element_type=F32),
        OWN,
    )


def halo_kernel(
    from_left, from_right, ends, sums, inflow, solid, weights, swap, rows,
    pay, edge, rates, near, far, turned, back, held,
):
    first = lax.axis_index("space") * COLS
    last = COLS * 16 - 1
    for side, ref, start in ((0, from_left, 2), (1, from_right, 0)):
        for r in range(ROWS):
            i = r * 2 + side
            for j, (at, n) in enumerate(CHUNKS):
                value = ref[r * 8 + j][:, :n]
                near[i, :, at : at + n] = value.astype(F32)
                held[i * MODES : (i + 1) * MODES, at : at + n] = value
            for j in range(3):
                at, n = CHUNKS[start + j]
                far[i, :, at : at + n] = ref[r * 8 + 5 + j][:, :n].astype(F32)
    for (at, n), part in zip(CHUNKS, turn(held, 64, swap)):
        turned[:, :, at : at + n] = part.reshape(4, MODES, n)
    for (at, n), part in zip(CHUNKS, reverse(held, 64, swap)):
        back[:, :, at : at + n] = part.reshape(4, MODES, n)
    source = inflow[...].astype(F32)
    for side, ref in ((0, from_left), (1, from_right)):
        for r in range(ROWS):
            i = r * 2 + side
            beyond = first - 1 if side == 0 else first + COLS
            column = jnp.clip(beyond, 1, last - 1)
            extra = ref[r * 8 + 4].astype(F32)
            rate = extra[:, 64:65] + extra[:, 65:66] + extra[:, 66:67]
            flag = extra[:, 67:68]
            h = near[i]
            own = ends[i].astype(F32)
            bounced = back[i]
            left, right = (far[i], own) if side == 0 else (own, far[i])
            left = jnp.where(solid[r, column - 1] == 1, bounced, left)
            right = jnp.where(solid[r, column + 1] == 1, bounced, right)
            outside = jnp.where(flag < 0.5, h, jnp.where(flag < 1.5, source, turned[i]))
            inside = jnp.where(solid[1 - r, column] == 1, bounced, near[(1 - r) * 2 + side])
            below, above = (outside, inside) if r == 0 else (inside, outside)
            value = h - rate * h + advection(None, rows, h, left, right, below, above)
            fluid = solid[r, column] == 0
            edge[4 + i] = jnp.where(fluid, value, 0.0)
            rates[i] = jnp.broadcast_to(jnp.where(fluid, rate, 0.0), (MODES, 128))

            inner = first if side == 0 else first + COLS - 1
            inside_band = (beyond >= 0) & (beyond <= last)
            used = inside_band & (solid[r, jnp.clip(beyond, 0, last)] == 0) & (solid[r, inner] == 0)
            taken = rows[2:3, :] > 0.5 if side == 0 else rows[2:3, :] < 0.5
            value = jnp.where(taken, rows[0:1, :] * h, 0.0)
            value = jnp.where(used, value, 0.0)
            edge[i] = value
            hi = value.astype(BF16)
            held[64 + i * MODES : 80 + i * MODES, :] = hi
            held[128 + i * MODES : 144 + i * MODES, :] = (value - hi.astype(F32)).astype(BF16)
    edge[8] = jnp.zeros((MODES, V), F32)
    folded = jnp.dot(held[...], weights[...], preferred_element_type=F32)
    place = lanes((MODES, 128)) % 32
    added = folded[64:128] + folded[128:]
    later = sums[1]
    for i in range(4):
        cell = (i // 2) * COLS + (0 if i % 2 == 0 else COLS - 1)
        later += jnp.where(place == cell, added[i * MODES : (i + 1) * MODES], 0.0)
    row = lax.broadcasted_iota(jnp.int32, (64, 128), 0)
    lane = lanes((64, 128))
    chosen = ((lane % 32) // 4 == row % 8) & (lane % 4 == row // MODES)
    parts = jnp.where(chosen, folded[:64], 0.0)
    halves = []
    for half in (0, 8):
        total = sum(parts[i * MODES + half : i * MODES + half + 8] for i in range(4))
        halves.append(jnp.sum(total, 0, keepdims=True))
    ends_sums = jnp.concatenate(halves + [jnp.zeros((6, 128), F32)], 0)
    for d in range(16):
        pay[d, :16, :] = sums[0]
        pay[d, 16:32, :] = later
        pay[d, 32:40, :] = ends_sums


def exact_nt(value, table):
    total = None
    for piece in pieces(value)[:2]:
        part = lax.dot_general(piece, table, NT, preferred_element_type=F32)
        total = part if total is None else total + part
    return total


def set_parameters(par, at, sums):
    s0, s1, s2, s3 = sums
    n = s0.shape[0]
    rho = WEIGHT * s0
    mx = (WEIGHT * HALF) * s1
    my = (WEIGHT * HALF) * s2
    en = (WEIGHT * HALF * HALF) * (4.0 * s3 + s0)
    safe = jnp.maximum(rho, RHO_FLOOR)
    ux = mx / safe
    uy = my / safe
    temp = jnp.maximum(en / safe - 0.5 * (ux * ux + uy * uy), TEMP_FLOOR)
    par[0, at : at + n] = ux
    par[1, at : at + n] = uy
    par[2, at : at + n] = (-0.5 * LOG2E) / temp
    par[3, at : at + n] = safe / (2.0 * math.pi * temp)


def factors(par, cell):
    ux = par[0, pl.ds(cell, 1), :]
    uy = par[1, pl.ds(cell, 1), :]
    rate = par[2, pl.ds(cell, 1), :]
    scale = par[3, pl.ds(cell, 1), :]
    speed = lax.broadcasted_iota(jnp.int32, (VX, K), 0).astype(F32) * STEP - VMAX
    dx = speed - ux
    dy = speed - uy
    return scale * jnp.exp2(dx * dx * rate), jnp.exp2(dy * dy * rate)


def project(along_x, along_y, scaled, projection):
    for i in range(VX):
        scaled[MODES * i : MODES * (i + 1), :] = (projection * along_x[i : i + 1]).astype(BF16)
    out = lax.dot_general(scaled[...], along_y.astype(BF16), NT, preferred_element_type=F32)
    out = jnp.concatenate([out[MODES * i : MODES * (i + 1)] for i in range(VX)], 1)
    return out.astype(BF16).astype(F32)


def collide_kernel(
    gathered, basis, projection, base_far, edge_far, cells_far, rates, inflow,
    relax, flags, solid, swap_far, rows, order,
    out, slots, held, par, sums1, equil, base, edge, cells, swap, arrived, ready, written,
):
    copies = [
        pltpu.make_async_copy(source, target, arrived.at[i])
        for i, (source, target) in enumerate(
            ((base_far, base), (edge_far, edge), (cells_far, cells), (swap_far, swap))
        )
    ]
    for copy in copies:
        copy.start()
    first = lax.axis_index("space") * COLS
    mode = lax.axis_index("mode") * MODES
    mine = projection[pl.ds(pl.multiple_of(mode, MODES), MODES), :].astype(F32)
    now = gathered[:, :16, :].reshape(K, 128).T
    later = gathered[:, 16:32, :].reshape(K, 128).T
    spread = jnp.broadcast_to(gathered[:, 32:34, :].reshape(32, 1, 128), (32, 8, 128)).reshape(K, 128)
    of_mode = lax.broadcasted_iota(jnp.int32, (K, 128), 0) % 8
    spread = jnp.where((lanes((K, 128)) % 32) // 4 == of_mode, spread, 0.0).T
    node = exact_nt(now, basis[...])
    halo_node = exact_nt(spread, basis[...])
    set_parameters(par, 0, [node[32 * i : 32 * i + 32] for i in range(4)])
    halo_sums = []
    for i in range(4):
        eight = sum(halo_node[32 * i + 8 * j : 32 * i + 8 * j + 8] for j in range(4))
        halo_sums.append(eight + jnp.concatenate([eight[4:], eight[:4]], 0))
    set_parameters(par, 32, halo_sums)
    slots[INFLOW] = inflow[...].astype(F32)

    odd = (2 * lax.broadcasted_iota(jnp.int32, (VX, K), 0) - (VX - 1)).astype(F32)
    tri = (odd * odd - 1.0) * 0.125

    def sums_of(value):
        return (
            jnp.sum(value, 0, keepdims=True),
            jnp.sum(value * odd, 0, keepdims=True),
            jnp.sum(value * tri, 0, keepdims=True),
        )

    def first_cell(c, slot):
        for r in range(ROWS):
            cell = r * COLS + c
            along_x, along_y = factors(par, cell)
            coll = project(along_x, along_y, equil.at[slot + r], mine)
            fluid = solid[r, first + c] == 0
            rate = jnp.where(fluid, relax[r, c], 0.0)
            end = jnp.where(c == 0, r * 2, jnp.where(c == COLS - 1, r * 2 + 1, 8))
            section = (base[cell] + edge[end] + rate * coll).astype(BF16)
            slots[cell] = section.astype(F32)
            held[pl.ds(pl.multiple_of(cell * MODES, MODES), MODES), :] = section
            x0, x1, x2 = sums_of(along_x)
            y0, y1, y2 = sums_of(along_y)
            y0, y1, y2 = rate * y0, rate * y1, rate * y2
            sums1[pl.ds(cell, 1), :] = x0 * y0
            sums1[pl.ds(32 + cell, 1), :] = x1 * y0
            sums1[pl.ds(64 + cell, 1), :] = x0 * y1
            sums1[pl.ds(96 + cell, 1), :] = x2 * y0 + x0 * y2

    def first_stage(i, carry):
        for u in range(GROUP):
            first_cell(i * GROUP + u, u * ROWS)
        return carry

    for copy in copies:
        copy.wait()
    lax.fori_loop(0, COLS // GROUP, first_stage, 0)
    for side in range(2):
        for r in range(ROWS):
            cell = HALO + r * 2 + side
            rate = rates[r * 2 + side][:, :1]
            along_x, along_y = factors(par, cell)
            coll = project(along_x, along_y, equil.at[r * 2 + side], mine)
            slots[cell] = (edge[4 + r * 2 + side] + rate * coll).astype(BF16).astype(F32)

    mirrored(slots, held, OWN, swap)
    mixed = later + exact_nt(sums1[...], projection[...])
    node = exact_nt(mixed, basis[...])
    set_parameters(par, 0, [node[32 * i : 32 * i + 32] for i in range(4)])

    writes = []
    for r in range(ROWS):
        for c in range(COLS):
            cell = r * COLS + c
            column = first + c
            along_x, along_y = factors(par, cell)
            coll = project(along_x, along_y, equil.at[cell], mine)
            left, right, below, above = sources(r, c, column, flags, solid)
            h = slots[cell]
            moved = advection(
                slots, rows, h, slots[left], slots[right], slots[below], slots[above]
            )
            value = h + moved + relax[r, c] * (coll - h)
            before = cells[cell * MODES : (cell + 1) * MODES, :].astype(F32)
            value = 0.5 * before + 0.5 * value
            value = jnp.where(solid[r, column] == 0, value, 0.0)
            held[cell * MODES : (cell + 1) * MODES, :] = value.astype(BF16)
        top = r * COLS * MODES
        value = by_other(held[top : top + COLS * MODES, :], order)
        ready[:, r, :, :] = value.astype(BF16).reshape(MODES, COLS, V)
        write = pltpu.make_async_copy(ready.at[:, r], out.at[:, r], written.at[r])
        write.start()
        writes.append(write)
    for write in writes:
        write.wait()


def on_device(dist, relax, flags, solid, inflow, basis, projection):
    weights, swap, rows, order, pick = tables()
    vmem = pl.BlockSpec(memory_space=pltpu.VMEM)
    smem = pl.BlockSpec(memory_space=pltpu.SMEM)
    far = pl.BlockSpec(memory_space=pl.ANY)
    params = pltpu.CompilerParams(vmem_limit_bytes=LIMIT)

    to_left, to_right = pl.pallas_call(
        edges_kernel,
        out_shape=(
            jax.ShapeDtypeStruct((16, MODES, 128), BF16),
            jax.ShapeDtypeStruct((16, MODES, 128), BF16),
        ),
        in_specs=[vmem, smem, smem, vmem],
        out_specs=(vmem, vmem),
        compiler_params=params,
    )(dist, relax, flags, pick)
    count = lax.axis_size("space")
    from_left = lax.ppermute(to_right, "space", [(i, (i + 1) % count) for i in range(count)])
    from_right = lax.ppermute(to_left, "space", [((i + 1) % count, i) for i in range(count)])

    cells, ends, base, sums = pl.pallas_call(
        explicit_kernel,
        out_shape=(
            jax.ShapeDtypeStruct((OWN * MODES, V), BF16),
            jax.ShapeDtypeStruct((4, MODES, V), BF16),
            jax.ShapeDtypeStruct((OWN, MODES, V), F32),
            jax.ShapeDtypeStruct((2, MODES, 128), F32),
        ),
        in_specs=[vmem] * 2 + [smem] * 3 + [vmem] * 4,
        out_specs=(vmem, vmem, vmem, vmem),
        scratch_shapes=[
            pltpu.VMEM((SLOTS, MODES, V), F32),
            pltpu.VMEM((576, V), BF16),
            pltpu.VMEM((OWN * MODES, V), BF16),
            pltpu.VMEM((OWN * MODES, V), BF16),
        ],
        compiler_params=params,
        cost_estimate=pl.CostEstimate(
            flops=20_000_000_000, bytes_accessed=4_000_000, transcendentals=0
        ),
    )(dist, inflow, relax, flags, solid, weights, swap, rows, order)

    pay, edge, rates = pl.pallas_call(
        halo_kernel,
        out_shape=(
            jax.ShapeDtypeStruct((16, 40, 128), F32),
            jax.ShapeDtypeStruct((9, MODES, V), F32),
            jax.ShapeDtypeStruct((4, MODES, 128), F32),
        ),
        in_specs=[vmem] * 5 + [smem] + [vmem] * 3,
        out_specs=(vmem, vmem, vmem),
        scratch_shapes=[pltpu.VMEM((4, MODES, V), F32)] * 4
        + [
            pltpu.VMEM((192, V), BF16),
        ],
        compiler_params=pltpu.CompilerParams(vmem_limit_bytes=63 * 1024 * 1024 + 900 * 1024),
    )(from_left, from_right, ends, sums, inflow, solid, weights, swap, rows)
    gathered = lax.all_to_all(pay, "mode", split_axis=0, concat_axis=0, tiled=True)

    return pl.pallas_call(
        collide_kernel,
        out_shape=jax.ShapeDtypeStruct((MODES, ROWS, COLS, V), BF16),
        in_specs=[vmem] * 3 + [far] * 3 + [vmem] * 2 + [smem] * 3 + [far, vmem, vmem],
        out_specs=far,
        scratch_shapes=[
            pltpu.VMEM((SLOTS, MODES, V), F32),
            pltpu.VMEM((576, V), BF16),
            pltpu.VMEM((4, 40, K), F32),
            pltpu.VMEM((128, K), F32),
            pltpu.VMEM((2 * GROUP, VX * MODES, K), BF16),
            pltpu.VMEM((OWN, MODES, V), F32),
            pltpu.VMEM((9, MODES, V), F32),
            pltpu.VMEM((OWN * MODES, V), BF16),
            pltpu.VMEM((1152, 128), BF16),
            pltpu.SemaphoreType.DMA((4,)),
            pltpu.VMEM((MODES, ROWS, COLS, V), BF16),
            pltpu.SemaphoreType.DMA((ROWS,)),
        ],
        compiler_params=params,
    )(
        gathered, basis, projection, base, edge, cells, rates, inflow,
        relax, flags, solid, swap, rows, order,
    )


def solution(mesh):
    placed = (
        P("mode", None, "space", None),
        P(None, "space"),
        P(None, "space"),
        P(),
        P("mode", None),
        P(),
        P(),
    )
    return jax.shard_map(
        on_device,
        mesh=mesh,
        in_specs=placed,
        out_specs=P("mode", None, "space", None),
        check_vma=False,
    )
```
